32 devices in a mesh: dp: 16 (over z, y, x), tensor: 2 (over core).
Axes of the slice: x: 2, y: 2, z: 4, core: 2. Of those that a mesh axis runs over, the one named last changes fastest.
Arguments:
- residual: bfloat16 [16384, 1024], P(('dp', 'tensor')), may hold values from -6 to 6
- cotangent: bfloat16 [16384, 1024], P(('dp', 'tensor')), may hold values from -6 to 6
- segment: int32 [16384], P('dp'), may hold values from 0 to 3, as said below
- expand: float32 [1024, 2, 1536], P('dp', None, 'tensor'), may hold values from -0.1875 to 0.1875
- expand_first: float32 [1024, 2, 1536], P('dp', None, 'tensor'), may hold values from -28 to 28
- expand_second: float32 [1024, 2, 1536], P('dp', None, 'tensor'), may hold values from 49.152 to 819.2
- select: float32 [1024, 280], replicated, may hold values from -0.1875 to 0.1875
- select_first: float32 [1024, 280], replicated, may hold values from -28 to 28
- select_second: float32 [1024, 280], replicated, may hold values from 49.152 to 819.2
- attention: float32 [1024, 2, 384], P('dp', 'tensor'), may hold values from -0.1875 to 0.1875
- attention_moment_one: float32 [1024, 2, 384], P('dp', 'tensor'), may hold values from -28 to 28
- attention_moment_two: float32 [1024, 2, 384], P('dp', 'tensor'), may hold values from 49.152 to 819.2
- project: float32 [1536, 1024], P('tensor', 'dp'), may hold values from -0.15625 to 0.15625
- project_first: float32 [1536, 1024], P('tensor', 'dp'), may hold values from -80 to 80
- project_second: float32 [1536, 1024], P('tensor', 'dp'), may hold values from 491.52 to 8192
- combine: float32 [512, 1024], P('tensor', 'dp'), may hold values from -1 to 1
- combine_first: float32 [512, 1024], P('tensor', 'dp'), may hold values from -28 to 28
- combine_second: float32 [512, 1024], P('tensor', 'dp'), may hold values from 49.152 to 819.2
- widening: float32 [1024, 2, 2048], P('dp', None, 'tensor'), may hold values from -0.1875 to 0.1875
- widening_first: float32 [1024, 2, 2048], P('dp', None, 'tensor'), may hold values from -28 to 28
- widening_second: float32 [1024, 2, 2048], P('dp', None, 'tensor'), may hold values from 49.152 to 819.2
- narrowing: float32 [2048, 1024], P('tensor', 'dp'), may hold values from -0.125 to 0.125
- narrowing_first: float32 [2048, 1024], P('tensor', 'dp'), may hold values from -28 to 28
- narrowing_second: float32 [2048, 1024], P('tensor', 'dp'), may hold values from 49.152 to 819.2
- kernel: float32 [4, 1792], replicated, may hold values from -3 to 3
- kernel_first: float32 [4, 1792], replicated, may hold values from -28 to 28
- kernel_second: float32 [4, 1792], replicated, may hold values from 49.152 to 819.2
- scales: float32 [3584], replicated, may hold values from 0.5 to 1.5
- scales_first: float32 [3584], replicated, may hold values from -80 to 80
- scales_second: float32 [3584], replicated, may hold values from 491.52 to 8192
- decays: float32 [3, 24], replicated, may hold values from -5 to 1.5, as said below
- decays_first: float32 [3, 24], replicated, may hold values from -256 to 256
- decays_second: float32 [3, 24], replicated, may hold values from 4915.2 to 81920
Outputs:
- output: bfloat16 [16384, 1024], P(('dp', 'tensor'))
- gradient: float32 [16384, 1024], P(('dp', 'tensor'))
- expand_mean: float32 [1024, 2, 1536], P('dp', None, 'tensor')
- expand_square: float32 [1024, 2, 1536], P('dp', None, 'tensor')
- expand_update: float32 [1024, 2, 1536], P('dp', None, 'tensor')
- select_mean: float32 [1024, 280], replicated
- select_square: float32 [1024, 280], replicated
- select_update: float32 [1024, 280], replicated
- attention_mean: float32 [1024, 2, 384], P('dp', 'tensor')
- attention_square: float32 [1024, 2, 384], P('dp', 'tensor')
- attention_update: float32 [1024, 2, 384], P('dp', 'tensor')
- project_mean: float32 [1536, 1024], P('tensor', 'dp')
- project_square: float32 [1536, 1024], P('tensor', 'dp')
- project_update: float32 [1536, 1024], P('tensor', 'dp')
- combine_mean: float32 [512, 1024], P('tensor', 'dp')
- combine_square: float32 [512, 1024], P('tensor', 'dp')
- combine_update: float32 [512, 1024], P('tensor', 'dp')
- widening_mean: float32 [1024, 2, 2048], P('dp', None, 'tensor')
- widening_square: float32 [1024, 2, 2048], P('dp', None, 'tensor')
- widening_update: float32 [1024, 2, 2048], P('dp', None, 'tensor')
- narrowing_mean: float32 [2048, 1024], P('tensor', 'dp')
- narrowing_square: float32 [2048, 1024], P('tensor', 'dp')
- narrowing_update: float32 [2048, 1024], P('tensor', 'dp')
- kernel_mean: float32 [4, 1792], replicated
- kernel_square: float32 [4, 1792], replicated
- kernel_update: float32 [4, 1792], replicated
- scales_mean: float32 [3584], replicated
- scales_square: float32 [3584], replicated
- scales_update: float32 [3584], replicated
- decays_mean: float32 [3, 24], replicated
- decays_square: float32 [3, 24], replicated
- decays_update: float32 [3, 24], replicated
The draws below stay inside these ranges and needn't reach their ends.
Inputs may be any that keep to these rules, and one draw needn't show every extreme that they name: `segment`: each block of 1024 rows holds 4 whole sequences numbered 0 to 3 in order, none empty; sequence 1 holds rows 511 and 512 of its block. `decays`: row 0 lies in -3 to 1, row 1 in 0.5 to 1.5, row 2 in -5 to -1.
All inputs are finite; a program needn't handle non-finite values.
Results may differ from the reference program's by a relative error of at most 0.012.
The reference program's roundings to bfloat16 on the way count: a program that leaves them out, or rounds other values in their place, can miss the bound.
Values may be sent and summed in bfloat16 or wider, within the bound.
No kernel may reach another device: no remote copies, remote signals or barrier semaphores. Data moves between devices by JAX's collectives and lax.ppermute only.
A program may use at most 192 MiB of HBM per device.

```python
import math
import jax
import jax.numpy as jnp
from jax import lax

MODEL_WIDTH = 1024
HM = 24
PD = 64
NS = 128
KC = 4
HQ = 8
KEY_VALUE_HEADS = 2
HD = 64
FF = 2048
TOK = 1024
STEP = 10
DSSM = 1536
GROUP_COLUMNS = 384
BCDT = 280
TOKEN_TOTAL = 16384
N_DP = 16
N_TENSOR = 2


def draw_segment(key, part):
    key = jax.random.fold_in(key, 11)
    subkeys = jax.random.split(key, 3)
    first_cut = jax.random.randint(subkeys[0], (N_DP, 1), TOK // 16, TOK // 4)
    last_cut = jax.random.randint(subkeys[1], (N_DP, 1), 3 * TOK // 4, 15 * TOK // 16 + 1)
    middle_cut = jax.random.randint(subkeys[2], (N_DP, 1), TOK // 2 + 1, last_cut)
    position = jnp.arange(TOK, dtype=jnp.int32)[None, :]
    numbers = (position >= first_cut).astype(jnp.int32) + (position >= middle_cut).astype(jnp.int32) + (position >= last_cut).astype(jnp.int32)
    return numbers.reshape(N_DP * TOK)


def draw_decays(key, part):
    key = jax.random.fold_in(key, 5)
    subkeys = jax.random.split(key, 3)
    log_rates = jax.random.uniform(subkeys[0], (HM,), jnp.float32, -3.0, 1.0)
    skip_gains = jax.random.uniform(subkeys[1], (HM,), jnp.float32, 0.5, 1.5)
    step_bias = jax.random.uniform(subkeys[2], (HM,), jnp.float32, -5.0, -1.0)
    return jnp.stack([log_rates, skip_gains, step_bias])


def levels(stream_key, dims, cuts, low, top_value):
    loudness = 1.0
    for dim, parts in cuts:
        draws = jax.random.uniform(jax.random.fold_in(jax.random.fold_in(stream_key, 6), dim), (parts,), jnp.float32, low / len(cuts), top_value / len(cuts))
        loudness = loudness * jnp.repeat(jnp.exp(draws), dims[dim] // parts).reshape((-1,) + (1,) * (len(dims) - 1 - dim))
    return loudness


def centred(rng, extent, deviation, bound, cuts=(), held_as=jnp.bfloat16):
    array = jax.random.normal(rng, extent, jnp.float32) * deviation
    if len(cuts) > 0:
        array = levels(rng, extent, cuts, -0.22, 0.18) * array
    return jnp.clip(array, min=-bound, max=bound).astype(held_as)


def setup_inputs(seed: int = 0) -> dict:
    key_of = jax.random.split(jax.random.key(seed), 34)
    residual = centred(key_of[0], (TOKEN_TOTAL, MODEL_WIDTH), 1.0, 6.0, ((0, 32),))
    cotangent = centred(key_of[1], (TOKEN_TOTAL, MODEL_WIDTH), 1.0, 6.0, ((0, 32),))
    segment = draw_segment(jax.random.fold_in(key_of[33], 71), 0)
    expand = centred(key_of[3], (MODEL_WIDTH, 2, DSSM), MODEL_WIDTH ** -0.5, 0.1875, ((0, 16), (2, 2)), jnp.float32)
    expand_first = centred(key_of[4], (MODEL_WIDTH, 2, DSSM), (0.035 * TOKEN_TOTAL ** 0.5), 28.0, ((0, 16), (2, 2)), jnp.float32)
    expand_second = jnp.clip(jnp.exp(math.log(819.2) - 2.8134107 * jax.random.uniform(key_of[5], (MODEL_WIDTH, 2, DSSM), jnp.float32) ** levels(key_of[5], (MODEL_WIDTH, 2, DSSM), ((0, 16), (2, 2)), -0.2, 0.2)), 49.152, 819.2)
    select = centred(key_of[6], (MODEL_WIDTH, BCDT), MODEL_WIDTH ** -0.5, 0.1875, (), jnp.float32)
    select_first = centred(key_of[7], (MODEL_WIDTH, BCDT), (0.035 * TOKEN_TOTAL ** 0.5), 28.0, (), jnp.float32)
    select_second = jnp.clip(jnp.exp(jax.random.uniform(key_of[8], (MODEL_WIDTH, BCDT), jnp.float32, math.log(49.152), math.log(819.2))), 49.152, 819.2)
    attention = centred(key_of[9], (MODEL_WIDTH, KEY_VALUE_HEADS, GROUP_COLUMNS), MODEL_WIDTH ** -0.5, 0.1875, ((0, 16), (1, 2)), jnp.float32)
    attention_moment_one = centred(key_of[10], (MODEL_WIDTH, KEY_VALUE_HEADS, GROUP_COLUMNS), (0.035 * TOKEN_TOTAL ** 0.5), 28.0, ((0, 16), (1, 2)), jnp.float32)
    attention_moment_two = jnp.clip(jnp.exp(math.log(819.2) - 2.8134107 * jax.random.uniform(key_of[11], (MODEL_WIDTH, KEY_VALUE_HEADS, GROUP_COLUMNS), jnp.float32) ** levels(key_of[11], (MODEL_WIDTH, KEY_VALUE_HEADS, GROUP_COLUMNS), ((0, 16), (1, 2)), -0.2, 0.2)), 49.152, 819.2)
    project = centred(key_of[12], (DSSM, MODEL_WIDTH), DSSM ** -0.5, 0.15625, ((0, 2), (1, 16)), jnp.float32)
    project_first = centred(key_of[13], (DSSM, MODEL_WIDTH), (0.11 * TOKEN_TOTAL ** 0.5), 80.0, ((0, 2), (1, 16)), jnp.float32)
    project_second = jnp.clip(jnp.exp(math.log(8192.0) - 2.8134107 * jax.random.uniform(key_of[14], (DSSM, MODEL_WIDTH), jnp.float32) ** levels(key_of[14], (DSSM, MODEL_WIDTH), ((0, 2), (1, 16)), -0.2, 0.2)), 491.52, 8192.0)
    combine = centred(key_of[15], (HQ * HD, MODEL_WIDTH), (HQ * HD // 16) ** -0.5, 1.0, ((0, 2), (1, 16)), jnp.float32)
    combine_first = centred(key_of[16], (HQ * HD, MODEL_WIDTH), (0.035 * TOKEN_TOTAL ** 0.5), 28.0, ((0, 2), (1, 16)), jnp.float32)
    combine_second = jnp.clip(jnp.exp(math.log(819.2) - 2.8134107 * jax.random.uniform(key_of[17], (HQ * HD, MODEL_WIDTH), jnp.float32) ** levels(key_of[17], (HQ * HD, MODEL_WIDTH), ((0, 2), (1, 16)), -0.2, 0.2)), 49.152, 819.2)
    widening = centred(key_of[18], (MODEL_WIDTH, 2, FF), MODEL_WIDTH ** -0.5, 0.1875, ((0, 16), (2, 2)), jnp.float32)
    widening_first = centred(key_of[19], (MODEL_WIDTH, 2, FF), (0.035 * TOKEN_TOTAL ** 0.5), 28.0, ((0, 16), (2, 2)), jnp.float32)
    widening_second = jnp.clip(jnp.exp(math.log(819.2) - 2.8134107 * jax.random.uniform(key_of[20], (MODEL_WIDTH, 2, FF), jnp.float32) ** levels(key_of[20], (MODEL_WIDTH, 2, FF), ((0, 16), (2, 2)), -0.2, 0.2)), 49.152, 819.2)
    narrowing = centred(key_of[21], (FF, MODEL_WIDTH), FF ** -0.5, 0.125, ((0, 2), (1, 16)), jnp.float32)
    narrowing_first = centred(key_of[22], (FF, MODEL_WIDTH), (0.035 * TOKEN_TOTAL ** 0.5), 28.0, ((0, 2), (1, 16)), jnp.float32)
    narrowing_second = jnp.clip(jnp.exp(math.log(819.2) - 2.8134107 * jax.random.uniform(key_of[23], (FF, MODEL_WIDTH), jnp.float32) ** levels(key_of[23], (FF, MODEL_WIDTH), ((0, 2), (1, 16)), -0.2, 0.2)), 49.152, 819.2)
    kernel = centred(key_of[24], (KC, DSSM + 2 * NS), KC ** -0.5, 3.0, (), jnp.float32)
    kernel_first = centred(key_of[25], (KC, DSSM + 2 * NS), (0.035 * TOKEN_TOTAL ** 0.5), 28.0, (), jnp.float32)
    kernel_second = jnp.clip(jnp.exp(jax.random.uniform(key_of[26], (KC, DSSM + 2 * NS), jnp.float32, math.log(49.152), math.log(819.2))), 49.152, 819.2)
    scales = jnp.clip(1.0 + 0.1 * jax.random.normal(key_of[27], (2 * MODEL_WIDTH + DSSM,), jnp.float32), 0.5, 1.5)
    scales_first = centred(key_of[28], (2 * MODEL_WIDTH + DSSM,), (0.11 * TOKEN_TOTAL ** 0.5), 80.0, (), jnp.float32)
    scales_second = jnp.clip(jnp.exp(jax.random.uniform(key_of[29], (2 * MODEL_WIDTH + DSSM,), jnp.float32, math.log(491.52), math.log(8192.0))), 491.52, 8192.0)
    decays = draw_decays(jax.random.fold_in(key_of[33], 71), 0)
    decays_first = centred(key_of[31], (3, HM), (0.35 * TOKEN_TOTAL ** 0.5), 256.0, (), jnp.float32)
    decays_second = jnp.clip(jnp.exp(jax.random.uniform(key_of[32], (3, HM), jnp.float32, math.log(4915.2), math.log(81920.0))), 4915.2, 81920.0)
    return {"residual": residual, "cotangent": cotangent, "segment": segment, "expand": expand, "expand_first": expand_first, "expand_second": expand_second, "select": select, "select_first": select_first, "select_second": select_second, "attention": attention, "attention_moment_one": attention_moment_one, "attention_moment_two": attention_moment_two, "project": project, "project_first": project_first, "project_second": project_second, "combine": combine, "combine_first": combine_first, "combine_second": combine_second, "widening": widening, "widening_first": widening_first, "widening_second": widening_second, "narrowing": narrowing, "narrowing_first": narrowing_first, "narrowing_second": narrowing_second, "kernel": kernel, "kernel_first": kernel_first, "kernel_second": kernel_second, "scales": scales, "scales_first": scales_first, "scales_second": scales_second, "decays": decays, "decays_first": decays_first, "decays_second": decays_second}


EPSILON = 1e-05
ROPE_BASE = 10000.0
MASKED = -1e+30
BETA_ONE = 0.9
BETA_TWO = 0.95
ADAM_EPSILON = 1e-08
WEIGHT_DECAY = 0.1
RATE_MATRIX = 0.1
RATE_PROJECT = 0.08
RATE_COMBINE = 0.5
RATE_NARROWING = 0.07
RATE_KERNEL = 1.0
RATE_SCALES = 0.5
RATE_DECAYS = 1.0

@jax.custom_vjp
def reduced_precision(v):
    return lax.optimization_barrier(v.astype(jnp.bfloat16)).astype(jnp.float32)

@jax.custom_vjp
def reduced_backward(v):
    return v

def low_keep(v):
    return (reduced_precision(v), None)

def low_pass(kept, grad):
    return (grad,)

def back_keep(v):
    return (v, None)

def back_low(kept, grad):
    return (reduced_precision(grad),)
reduced_precision.defvjp(low_keep, low_pass)
reduced_backward.defvjp(back_keep, back_low)

def precise_product(left_side, right_side):
    return jnp.dot(left_side, right_side, precision=lax.Precision.HIGHEST)

def sigmoid_linear(values):
    return values * jax.nn.sigmoid(values)

def rms_apply(values, gain_vector):
    return values * lax.rsqrt(lax.optimization_barrier(jnp.mean(values * values, axis=-1, keepdims=True)) + EPSILON) * gain_vector

def token_places(segment):
    row_count = segment.shape[0]
    row_index = jnp.arange(row_count, dtype=jnp.int32)
    seq_edges = jnp.concatenate([jnp.ones((1,), bool), segment[1:] != segment[:-1]])
    seq_starts = lax.cummax(jnp.where(seq_edges, row_index, 0), axis=0)
    return row_index - seq_starts

def causal_filter(values, filter_taps, segment):
    summed = filter_taps[0] * values
    for offset in range(1, filter_taps.shape[0]):
        shifted = jnp.concatenate([jnp.zeros((offset, values.shape[1]), values.dtype), values[:-offset]], axis=0)
        earlier = jnp.concatenate([jnp.full((offset,), -1, jnp.int32), segment[:-offset]])
        summed = summed + filter_taps[offset] * jnp.where((earlier == segment)[:, None], shifted, 0.0)
    return summed

def ssm_mix(gate_part, inner, state_raw, step_raw, taps_inner, taps_state, log_rates, skip_gains, step_bias, segment):
    row_count = inner.shape[0]
    mixed_inner = sigmoid_linear(causal_filter(inner, taps_inner, segment))
    states = sigmoid_linear(causal_filter(state_raw, taps_state, segment))
    inputs_b = states[:, :NS]
    readout = states[:, NS:]
    step_sizes = jax.nn.softplus(step_raw + step_bias)
    rates = -jnp.exp(log_rates) * step_sizes
    running = jnp.cumsum(rates, axis=0)
    row_index = jnp.arange(row_count, dtype=jnp.int32)
    allowed = (segment[:, None] == segment[None, :]) & (row_index[:, None] >= row_index[None, :])
    coupling = precise_product(readout, inputs_b.T)
    heads_n = step_sizes.shape[1]
    per_head = mixed_inner.reshape(row_count, heads_n, PD)

    def one_head(pieces):
        run_head, step_head, value_head = pieces
        decay_gap = jnp.where(allowed, run_head[:, None] - run_head[None, :], MASKED)
        return precise_product(coupling * jnp.exp(decay_gap), step_head[:, None] * value_head)
    outputs = lax.map(jax.checkpoint(one_head), (running.T, step_sizes.T, per_head.transpose(1, 0, 2)))
    result = outputs.transpose(1, 0, 2) + skip_gains[None, :, None] * per_head
    return result.reshape(row_count, heads_n * PD) * sigmoid_linear(gate_part)

def rotate(values, token_positions):
    halfsize = HD // 2
    frequency = ROPE_BASE ** (-jnp.arange(halfsize, dtype=jnp.float32) * 2.0 / HD)
    angles = token_positions.astype(jnp.float32)[:, None] * frequency[None, :]
    cosine = jnp.cos(angles)[:, None, :]
    sine_table = jnp.sin(angles)[:, None, :]
    first_half = values[..., :halfsize]
    second_half = values[..., halfsize:]
    return jnp.concatenate([first_half * cosine - second_half * sine_table, second_half * cosine + first_half * sine_table], axis=-1)

def attend_head_group(packed_tokens, token_positions, segment):
    row_count = packed_tokens.shape[0]
    groups = packed_tokens.shape[1] // HD - 2
    queries = rotate(packed_tokens[:, :groups * HD].reshape(row_count, groups, HD), token_positions)
    key_rows = rotate(packed_tokens[:, groups * HD:(groups + 1) * HD].reshape(row_count, 1, HD), token_positions)[:, 0]
    value_rows = packed_tokens[:, (groups + 1) * HD:]
    row_index = jnp.arange(row_count, dtype=jnp.int32)
    allowed = (segment[:, None] == segment[None, :]) & (row_index[:, None] >= row_index[None, :])
    score_scale = 1.0 / math.sqrt(HD)

    def one_head(query_head):
        scores = jnp.where(allowed, precise_product(query_head, key_rows.T) * score_scale, MASKED)
        row_peak = lax.optimization_barrier(jnp.max(scores, axis=1, keepdims=True))
        weights = jnp.exp(scores - row_peak)
        return precise_product(weights, value_rows) / lax.optimization_barrier(jnp.sum(weights, axis=1, keepdims=True))
    outputs = lax.map(jax.checkpoint(one_head), queries.transpose(1, 0, 2))
    return outputs.transpose(1, 0, 2).reshape(row_count, groups * HD)

def layer(block_rows, segment, expand, select, attention, project, combine, widening, narrowing, kernel, scales, decays):
    token_positions = token_places(segment)
    normed_input = reduced_precision(rms_apply(block_rows, scales[:MODEL_WIDTH]))
    expanded = reduced_backward(precise_product(normed_input, reduced_precision(expand).reshape(MODEL_WIDTH, 2 * DSSM)))
    packed_tokens = reduced_backward(precise_product(normed_input, reduced_precision(attention).reshape(MODEL_WIDTH, KEY_VALUE_HEADS * GROUP_COLUMNS)))
    select_low = reduced_precision(select)
    heads_group = HM // N_TENSOR
    width_group = DSSM // N_TENSOR
    gated_parts = []
    for head_group in range(N_TENSOR):
        selected = reduced_backward(precise_product(normed_input, select_low))
        low_col = head_group * width_group
        low_head = head_group * heads_group
        gated_parts.append(ssm_mix(expanded[:, low_col:low_col + width_group], expanded[:, DSSM + low_col:DSSM + low_col + width_group], selected[:, :2 * NS], selected[:, 2 * NS + low_head:2 * NS + low_head + heads_group], kernel[:, low_col:low_col + width_group], kernel[:, DSSM:], decays[0, low_head:low_head + heads_group], decays[1, low_head:low_head + heads_group], decays[2, low_head:low_head + heads_group], segment))
    gated = jnp.concatenate(gated_parts, axis=1)
    inner_normed = reduced_precision(rms_apply(gated, scales[2 * MODEL_WIDTH:]))
    attention_result = reduced_precision(jnp.concatenate([attend_head_group(packed_tokens[:, key_value_slot * GROUP_COLUMNS:(key_value_slot + 1) * GROUP_COLUMNS], token_positions, segment) for key_value_slot in range(KEY_VALUE_HEADS)], axis=1))
    mixed_out = reduced_backward(precise_product(inner_normed, reduced_precision(project)) + precise_product(attention_result, reduced_precision(combine)))
    hidden = block_rows + mixed_out
    normed_two = reduced_precision(rms_apply(hidden, scales[MODEL_WIDTH:2 * MODEL_WIDTH]))
    gate_up = reduced_backward(precise_product(normed_two, reduced_precision(widening).reshape(MODEL_WIDTH, 2 * FF)))
    activated = reduced_precision(sigmoid_linear(gate_up[:, :FF]) * gate_up[:, FF:])
    return hidden + reduced_backward(precise_product(activated, reduced_precision(narrowing)))

def adam_step(weight_array, gradient_sum, first_moment, second_moment, rate, decay_rate):
    first_new = BETA_ONE * first_moment + (1.0 - BETA_ONE) * gradient_sum
    second_new = BETA_TWO * second_moment + (1.0 - BETA_TWO) * gradient_sum * gradient_sum
    scaled = first_new / (1.0 - BETA_ONE ** STEP) / (jnp.sqrt(second_new / (1.0 - BETA_TWO ** STEP)) + ADAM_EPSILON)
    return (first_new, second_new, weight_array - rate * (scaled + decay_rate * weight_array))

def reference(residual, cotangent, segment, expand, expand_first, expand_second, select, select_first, select_second, attention, attention_moment_one, attention_moment_two, project, project_first, project_second, combine, combine_first, combine_second, widening, widening_first, widening_second, narrowing, narrowing_first, narrowing_second, kernel, kernel_first, kernel_second, scales, scales_first, scales_second, decays, decays_first, decays_second):
    params = (expand, select, attention, project, combine, widening, narrowing, kernel, scales, decays)
    blocks = (residual.astype(jnp.float32).reshape(N_DP, TOK, MODEL_WIDTH), cotangent.astype(jnp.float32).reshape(N_DP, TOK, MODEL_WIDTH), segment.reshape(N_DP, TOK))

    def accumulate(totals, block_data):
        block_rows, block_cot, block_segment = block_data

        def forward(rows_in, *weight_list):
            return layer(rows_in, block_segment, *weight_list)
        produced, pullback = jax.vjp(forward, block_rows, *params)
        grads = pullback(block_cot)
        return (tuple((running_total + gradient_part for running_total, gradient_part in zip(totals, grads[1:]))), (produced, grads[0]))
    initial = tuple((jnp.zeros_like(weight_array) for weight_array in params))
    totals, (produced, back_rows) = lax.scan(accumulate, initial, blocks)
    output = produced.reshape(TOKEN_TOTAL, MODEL_WIDTH).astype(jnp.bfloat16)
    gradient = back_rows.reshape(TOKEN_TOTAL, MODEL_WIDTH)
    expand_mean, expand_square, expand_update = adam_step(expand, totals[0], expand_first, expand_second, RATE_MATRIX, WEIGHT_DECAY)
    select_mean, select_square, select_update = adam_step(select, totals[1], select_first, select_second, RATE_MATRIX, WEIGHT_DECAY)
    attention_mean, attention_square, attention_update = adam_step(attention, totals[2], attention_moment_one, attention_moment_two, RATE_MATRIX, WEIGHT_DECAY)
    project_mean, project_square, project_update = adam_step(project, totals[3], project_first, project_second, RATE_PROJECT, WEIGHT_DECAY)
    combine_mean, combine_square, combine_update = adam_step(combine, totals[4], combine_first, combine_second, RATE_COMBINE, WEIGHT_DECAY)
    widening_mean, widening_square, widening_update = adam_step(widening, totals[5], widening_first, widening_second, RATE_MATRIX, WEIGHT_DECAY)
    narrowing_mean, narrowing_square, narrowing_update = adam_step(narrowing, totals[6], narrowing_first, narrowing_second, RATE_NARROWING, WEIGHT_DECAY)
    kernel_mean, kernel_square, kernel_update = adam_step(kernel, totals[7], kernel_first, kernel_second, RATE_KERNEL, 0.0)
    scales_mean, scales_square, scales_update = adam_step(scales, totals[8], scales_first, scales_second, RATE_SCALES, 0.0)
    decays_mean, decays_square, decays_update = adam_step(decays, totals[9], decays_first, decays_second, RATE_DECAYS, 0.0)
    return (output, gradient, expand_mean, expand_square, expand_update, select_mean, select_square, select_update, attention_mean, attention_square, attention_update, project_mean, project_square, project_update, combine_mean, combine_square, combine_update, widening_mean, widening_square, widening_update, narrowing_mean, narrowing_square, narrowing_update, kernel_mean, kernel_square, kernel_update, scales_mean, scales_square, scales_update, decays_mean, decays_square, decays_update)
```

```python
import math

import jax
import jax.numpy as jnp
from jax import lax
from jax.experimental import pallas as pl
from jax.experimental.pallas import tpu as pltpu
from jax.sharding import PartitionSpec as P

MODEL_WIDTH = 1024
PD = 64
NS = 128
HD = 64
STEP = 10
DSSM = 1536
GROUP_COLUMNS = 384
KC = 4


EPSILON = 1e-05
ROPE_BASE = 10000.0
MASKED = -1e30
BETA_ONE = 0.9
BETA_TWO = 0.95
ADAM_EPSILON = 1e-08
WEIGHT_DECAY = 0.1
RATE_MATRIX = 0.1
RATE_PROJECT = 0.08
RATE_COMBINE = 0.5
RATE_NARROWING = 0.07
RATE_KERNEL = 1.0
RATE_SCALES = 0.5
RATE_DECAYS = 1.0


def product(left_side, right_side):
    return jnp.dot(left_side, right_side, preferred_element_type=jnp.float32)


def product_nt(left_side, right_side):
    return lax.dot_general(
        left_side, right_side, (((1,), (1,)), ((), ())), preferred_element_type=jnp.float32
    )


def product_tn(left_side, right_side):
    return lax.dot_general(
        left_side, right_side, (((0,), (0,)), ((), ())), preferred_element_type=jnp.float32
    )


def sigmoid_linear(values):
    return values * jax.nn.sigmoid(values)


def rms_apply(values, gain_vector):
    return (
        values
        * lax.rsqrt(jnp.mean(values * values, axis=-1, keepdims=True) + EPSILON)
        * gain_vector
    )


def token_places(segment):
    row_count = segment.shape[0]
    row_index = jnp.arange(row_count, dtype=jnp.int32)
    seq_edges = jnp.concatenate([jnp.ones((1,), bool), segment[1:] != segment[:-1]])
    seq_starts = lax.cummax(jnp.where(seq_edges, row_index, 0), axis=0)
    return row_index - seq_starts


CHUNK = 256
HEAD_ROWS = 8


def dot_nn(a, b):
    return jnp.dot(a, b, preferred_element_type=jnp.float32)


def dot_nt(a, b):
    return lax.dot_general(a, b, (((1,), (1,)), ((), ())), preferred_element_type=jnp.float32)


def dot_tn(a, b):
    return lax.dot_general(a, b, (((0,), (0,)), ((), ())), preferred_element_type=jnp.float32)


def low_of(values):
    return values.astype(jnp.bfloat16)


def two_of(values):
    high = values.astype(jnp.bfloat16)
    return high, (values - high.astype(jnp.float32)).astype(jnp.bfloat16)


def fine(dot, a, b):
    a_high, a_low = two_of(a)
    b_high, b_low = two_of(b)
    return dot(a_high, b_high) + (dot(a_high, b_low) + dot(a_low, b_high))


def fine_left(dot, a, exact):
    a_high, a_low = two_of(a)
    return dot(a_high, exact) + dot(a_low, exact)


def fine_right(dot, exact, b):
    b_high, b_low = two_of(b)
    b_rest = b - b_high.astype(jnp.float32) - b_low.astype(jnp.float32)
    return dot(exact, b_high) + (dot(exact, b_low) + dot(exact, b_rest.astype(jnp.bfloat16)))


def allowed_pairs(seg_col, seg_row, row_start):
    rows, columns = seg_col.shape[0], seg_row.shape[1]
    row_index = lax.broadcasted_iota(jnp.int32, (rows, columns), 0) + row_start
    column_index = lax.broadcasted_iota(jnp.int32, (rows, columns), 1)
    return (seg_col == seg_row) & (row_index >= column_index)


def swap_halves(values):
    width = values.shape[1]
    lane = lax.broadcasted_iota(jnp.int32, values.shape, 1)
    after = pltpu.roll(values, width - HD // 2, 1)
    before = pltpu.roll(values, HD // 2, 1)
    return jnp.where(lane % HD < HD // 2, after, before)


def turn_parts(cosine_ref, sine_ref, heads):
    scale = 1.0 / math.sqrt(HD)
    cosine, sine = cosine_ref[...], sine_ref[...]
    is_key = lax.broadcasted_iota(jnp.int32, cosine.shape, 1) < HD
    for h in range(0, heads, 2):
        yield slice(h * HD, (h + 2) * HD), cosine * scale, sine * scale
    yield (
        slice(heads * HD, (heads + 2) * HD),
        jnp.where(is_key, cosine, 1.0),
        jnp.where(is_key, sine, 0.0),
    )


def attend_kernel(packed_ref, cosine_ref, sine_ref, col_ref, row_ref, out_ref, rotated_ref, peak_ref):
    heads = out_ref.shape[1] // HD
    for at, cosine, sine in turn_parts(cosine_ref, sine_ref, heads):
        values = packed_ref[:, at]
        rotated_ref[:, at] = low_of(values * cosine + swap_halves(values) * sine)
    for start in range(0, out_ref.shape[0], CHUNK):
        stop = start + CHUNK
        mask = allowed_pairs(col_ref[start:stop, :], row_ref[:, :stop], start)
        keys = rotated_ref[:stop, heads * HD : (heads + 1) * HD]
        value_rows = rotated_ref[:stop, (heads + 1) * HD :]
        for h in range(heads):
            query = rotated_ref[start:stop, h * HD : (h + 1) * HD]
            scores = jnp.where(mask, dot_nt(query, keys), MASKED)
            peak = jnp.max(scores, axis=1, keepdims=True)
            weights = jnp.exp(scores - peak)
            total = jnp.sum(weights, axis=1, keepdims=True)
            out_ref[start:stop, h * HD : (h + 1) * HD] = low_of(
                dot_nn(low_of(weights), value_rows) / total
            )
            peak_ref[start:stop, h : h + 1] = peak + jnp.log(total)


def attend_back_kernel(
    rotated_ref, peak_ref, grad_ref, cosine_ref, sine_ref, col_ref, row_ref, out_ref, acc_ref
):
    heads = grad_ref.shape[1] // HD
    at_key, at_value = heads * HD, (heads + 1) * HD
    acc_ref[:, at_key:] = jnp.zeros((acc_ref.shape[0], 2 * HD), jnp.float32)
    for start in range(0, grad_ref.shape[0], CHUNK):
        stop = start + CHUNK
        mask = allowed_pairs(col_ref[start:stop, :], row_ref[:, :stop], start)
        keys = rotated_ref[:stop, at_key:at_value]
        value_rows = rotated_ref[:stop, at_value:]
        d_keys = jnp.zeros((stop, HD), jnp.float32)
        d_values = jnp.zeros((stop, HD), jnp.float32)
        for h in range(heads):
            query = rotated_ref[start:stop, h * HD : (h + 1) * HD]
            grad = low_of(grad_ref[start:stop, h * HD : (h + 1) * HD])
            scores = jnp.where(mask, dot_nt(query, keys), MASKED)
            weights = jnp.exp(scores - peak_ref[start:stop, h : h + 1])
            d_weights = dot_nt(grad, value_rows)
            mean = jnp.sum(weights * d_weights, axis=1, keepdims=True)
            d_scores = low_of(weights * (d_weights - mean))
            acc_ref[start:stop, h * HD : (h + 1) * HD] = dot_nn(d_scores, keys)
            d_keys = d_keys + dot_tn(d_scores, query)
            d_values = d_values + dot_tn(low_of(weights), grad)
        acc_ref[:stop, at_key:at_value] += d_keys
        acc_ref[:stop, at_value:] += d_values
    for at, cosine, sine in turn_parts(cosine_ref, sine_ref, heads):
        grads = acc_ref[:, at]
        out_ref[:, at] = low_of(grads * cosine + swap_halves(grads * sine))


def whole_call(kernel, out_shape, scratch_shapes=()):
    return pl.pallas_call(
        kernel,
        out_shape=out_shape,
        scratch_shapes=list(scratch_shapes),
        compiler_params=pltpu.CompilerParams(vmem_limit_bytes=48 * 1024 * 1024),
    )


def attend_forward(packed, cosine, sine, seg_col, seg_row):
    rows, columns = packed.shape
    heads = columns // HD - 2
    return whole_call(
        attend_kernel,
        (
            jax.ShapeDtypeStruct((rows, heads * HD), jnp.bfloat16),
            jax.ShapeDtypeStruct((rows, columns), jnp.bfloat16),
            jax.ShapeDtypeStruct((rows, heads), jnp.float32),
        ),
    )(packed, cosine, sine, seg_col, seg_row)


def attend_backward(rotated, peaks, grad, cosine, sine, seg_col, seg_row):
    rows, columns = rotated.shape
    return whole_call(
        attend_back_kernel,
        jax.ShapeDtypeStruct((rows, columns), jnp.bfloat16),
        [pltpu.VMEM((rows, columns), jnp.float32)],
    )(rotated, peaks, grad, cosine, sine, seg_col, seg_row)


def rotary_tables(places):
    halfsize = HD // 2
    lane = jnp.arange(2 * HD, dtype=jnp.int32) % HD
    frequency = ROPE_BASE ** (-(lane % halfsize).astype(jnp.float32) * 2.0 / HD)
    angles = places.astype(jnp.float32)[:, None] * frequency[None, :]
    return jnp.cos(angles), jnp.where(lane < halfsize, -1.0, 1.0)[None, :] * jnp.sin(angles)


def spread_matrix(heads):
    row = lax.broadcasted_iota(jnp.int32, (heads, heads * PD), 0)
    column = lax.broadcasted_iota(jnp.int32, (heads, heads * PD), 1)
    return jnp.where(column // PD == row, 1.0, 0.0).astype(jnp.bfloat16)


def spread_row(values, spread):
    return fine_left(dot_nn, jnp.broadcast_to(values, (8, values.shape[1])), spread)[:1]


def chunk_decays(dt_ref, dt_row_ref, rate_ref, rate_row_ref, in_ref, out_ref):
    rows = dt_ref.shape[0]
    row = lax.broadcasted_iota(jnp.int32, (rows, rows), 0)
    column = lax.broadcasted_iota(jnp.int32, (rows, rows), 1)
    lower = jnp.where(row >= column, 1.0, 0.0).astype(jnp.bfloat16)
    dt = dt_ref[...]
    running = fine_right(dot_nn, lower, dt * rate_ref[...])
    rate_rows = dt_row_ref[...] * rate_row_ref[...]
    high, mid = two_of(rate_rows)
    rest = low_of(rate_rows - high.astype(jnp.float32) - mid.astype(jnp.float32))
    running_row = dot_nt(high, lower) + (dot_nt(mid, lower) + dot_nt(rest, lower))
    last = running[rows - 1 :, :]
    entering = jnp.exp(running) * in_ref[...]
    leaving = jnp.exp(last - running) * out_ref[...]
    keep = jnp.exp(last) * in_ref[rows - 1 :, :]
    return lower, dt, running, running_row, entering, leaving, keep


def filtered(rows_ref, values, taps_ref, places):
    rows = values.shape[0]
    rows_ref[HEAD_ROWS:, :] = values
    summed = taps_ref[0:1, :] * values
    for k in range(1, taps_ref.shape[0]):
        shifted = rows_ref[HEAD_ROWS - k : HEAD_ROWS - k + rows, :]
        summed = summed + taps_ref[k : k + 1, :] * jnp.where(places >= k, shifted, 0.0)
    rows_ref[:HEAD_ROWS, :] = rows_ref[rows:, :]
    return summed


def filter_back(rows_ref, values, grad, taps_ref, places_ref, d_taps_ref):
    rows = values.shape[0]
    rows_ref[:rows, :] = grad
    d_taps_ref[0:1, :] += jnp.sum(values * grad, axis=0, keepdims=True)
    d_values = taps_ref[0:1, :] * grad
    for k in range(1, taps_ref.shape[0]):
        shifted = jnp.where(places_ref[k : k + rows, :] >= k, rows_ref[k : k + rows, :], 0.0)
        d_values = d_values + taps_ref[k : k + 1, :] * shifted
        d_taps_ref[k : k + 1, :] += jnp.sum(values * shifted, axis=0, keepdims=True)
    rows_ref[rows:, :] = rows_ref[:HEAD_ROWS, :]
    return d_values


def slope(values):
    sigmoid = jax.nn.sigmoid(values)
    return sigmoid * (1.0 + values * (1.0 - sigmoid))


def ssd_kernel(
    inner_ref, raw_ref, taps_inner_ref, taps_state_ref, skip_ref,
    dt_ref, dt_row_ref, rate_ref, rate_row_ref, col_ref, row_ref, in_ref, out_mask_ref, places_ref,
    gate_ref,
    gated_ref, y_ref, squares_ref, pre_inner_ref, pre_state_ref, kept_ref,
    state_ref, inner_rows_ref, state_rows_ref,
):
    @pl.when(pl.program_id(0) == 0)
    def _():
        state_ref[...] = jnp.zeros_like(state_ref)
        inner_rows_ref[:HEAD_ROWS, :] = jnp.zeros((HEAD_ROWS, inner_rows_ref.shape[1]), jnp.float32)
        state_rows_ref[:HEAD_ROWS, :] = jnp.zeros((HEAD_ROWS, state_rows_ref.shape[1]), jnp.float32)

    heads = dt_ref.shape[1]
    spread = spread_matrix(heads)
    _, dt, running, running_row, entering, leaving, keep = chunk_decays(
        dt_ref, dt_row_ref, rate_ref, rate_row_ref, in_ref, out_mask_ref
    )
    places = places_ref[...]
    pre_inner = filtered(inner_rows_ref, inner_ref[...], taps_inner_ref, places)
    pre_state = filtered(state_rows_ref, raw_ref[...], taps_state_ref, places)
    pre_inner_ref[...] = pre_inner
    pre_state_ref[...] = pre_state
    mixed = sigmoid_linear(pre_inner)
    states = sigmoid_linear(pre_state)
    inputs_b, readout = states[:, :NS], states[:, NS:]
    mask = allowed_pairs(col_ref[...], row_ref[...], 0)
    scaled = mixed * fine_left(dot_nn, dt, spread)
    scaled_low = low_of(scaled)
    coupling = jnp.where(mask, fine(dot_nt, readout, inputs_b), 0.0)
    state = state_ref[...]
    kept_ref[0] = state
    y_ref[...] = skip_ref[...] * mixed + fine(dot_nn, readout, state) * fine_left(
        dot_nn, entering, spread
    )
    for h in range(heads):
        gap = jnp.where(mask, running[:, h : h + 1] - running_row[h : h + 1, :], MASKED)
        weights = low_of(coupling * jnp.exp(gap))
        y_ref[:, h * PD : (h + 1) * PD] += dot_nn(weights, scaled_low[:, h * PD : (h + 1) * PD])
    gated = y_ref[...] * sigmoid_linear(gate_ref[...])
    gated_ref[...] = gated
    squares_ref[...] = jnp.sum(gated * gated, axis=1, keepdims=True)
    state_ref[...] = state * spread_row(keep, spread) + fine(
        dot_tn, inputs_b, scaled * fine_left(dot_nn, leaving, spread)
    )


def ssd_back_kernel(
    inner_ref, raw_ref, taps_inner_ref, taps_state_ref, skip_ref,
    dt_ref, dt_row_ref, rate_ref, rate_row_ref, col_ref, row_ref, in_ref, out_mask_ref, places_ref,
    pre_inner_ref, pre_state_ref, kept_ref, grad_ref,
    d_inner_ref, d_raw_ref, d_dt_ref, d_rate_ref, d_taps_inner_ref, d_taps_state_ref, d_skip_ref,
    carry_ref, within_ref, d_scaled_ref, inner_rows_ref, state_rows_ref, place_rows_ref,
):
    rows, heads = dt_ref.shape

    @pl.when(pl.program_id(0) == 0)
    def _():
        carry_ref[...] = jnp.zeros_like(carry_ref)
        d_taps_inner_ref[...] = jnp.zeros_like(d_taps_inner_ref)
        d_taps_state_ref[...] = jnp.zeros_like(d_taps_state_ref)
        d_skip_ref[...] = jnp.zeros_like(d_skip_ref)
        inner_rows_ref[rows:, :] = jnp.zeros((HEAD_ROWS, inner_rows_ref.shape[1]), jnp.float32)
        state_rows_ref[rows:, :] = jnp.zeros((HEAD_ROWS, state_rows_ref.shape[1]), jnp.float32)
        place_rows_ref[rows:, :] = jnp.zeros((HEAD_ROWS, 1), jnp.int32)

    spread = spread_matrix(heads)
    lower, dt, running, running_row, entering, leaving, keep = chunk_decays(
        dt_ref, dt_row_ref, rate_ref, rate_row_ref, in_ref, out_mask_ref
    )
    mask = allowed_pairs(col_ref[...], row_ref[...], 0)
    pre_inner, pre_state = pre_inner_ref[...], pre_state_ref[...]
    mixed = sigmoid_linear(pre_inner)
    states = sigmoid_linear(pre_state)
    inputs_b, readout = states[:, :NS], states[:, NS:]
    dt_spread = fine_left(dot_nn, dt, spread)
    scaled = mixed * dt_spread
    scaled_low = low_of(scaled)
    grad = grad_ref[...]
    grad_low = low_of(grad)
    coupling = jnp.where(mask, fine(dot_nt, readout, inputs_b), 0.0)
    d_coupling = jnp.zeros_like(coupling)
    for h in range(heads):
        at = slice(h * PD, (h + 1) * PD)
        gap = jnp.where(mask, running[:, h : h + 1] - running_row[h : h + 1, :], MASKED)
        decay = jnp.exp(gap)
        weights = low_of(coupling * decay)
        d_coupling = d_coupling + dot_nt(grad_low[:, at], scaled_low[:, at]) * decay
        d_scaled_ref[:, at] = dot_tn(weights, grad_low[:, at])
        within_ref[:, at] = dot_nn(weights, scaled_low[:, at])
    state = kept_ref[0]
    carry = carry_ref[...]
    entering_spread = fine_left(dot_nn, entering, spread)
    leaving_spread = fine_left(dot_nn, leaving, spread)
    keep_spread = spread_row(keep, spread)
    grad_in = grad * entering_spread
    scaled_out = scaled * leaving_spread
    from_state = fine(dot_nn, readout, state) * grad_in
    d_scaled_state = fine(dot_nn, inputs_b, carry) * leaving_spread
    to_state = scaled * d_scaled_state
    d_scaled_within = d_scaled_ref[...]
    own = grad_low.astype(jnp.float32) * within_ref[...]
    own = own - scaled_low.astype(jnp.float32) * d_scaled_within
    d_running = fine_left(dot_nt, own + from_state - to_state, spread)
    at_end = jnp.sum(to_state, axis=0, keepdims=True) + keep_spread * jnp.sum(
        carry * state, axis=0, keepdims=True
    )
    at_end = fine_left(dot_nt, jnp.broadcast_to(at_end, (8, at_end.shape[1])), spread)[:1]
    d_high, d_rest = two_of(d_running)
    d_rate = dot_tn(lower, d_high) + dot_tn(lower, d_rest) + at_end
    d_scaled = d_scaled_within + d_scaled_state
    d_dt_ref[...] = fine_left(dot_nt, d_scaled * mixed, spread) + d_rate * rate_ref[...]
    d_rate_ref[0] = jnp.sum(d_rate * dt, axis=0, keepdims=True)
    d_skip_ref[...] += jnp.sum(grad * mixed, axis=0, keepdims=True)
    d_mixed = d_scaled * dt_spread + skip_ref[...] * grad
    d_inputs = fine(dot_tn, d_coupling, readout) + fine(dot_nt, scaled_out, carry)
    d_readout = fine(dot_nn, d_coupling, inputs_b) + fine(dot_nt, grad_in, state)
    carry_ref[...] = carry * keep_spread + fine(dot_tn, readout, grad_in)
    place_rows_ref[:rows, :] = places_ref[...]
    d_inner_ref[...] = low_of(
        filter_back(
            inner_rows_ref, inner_ref[...], d_mixed * slope(pre_inner), taps_inner_ref,
            place_rows_ref, d_taps_inner_ref,
        )
    )
    d_states = jnp.concatenate([d_inputs, d_readout], axis=1) * slope(pre_state)
    d_raw_ref[...] = low_of(
        filter_back(
            state_rows_ref, raw_ref[...], d_states, taps_state_ref, place_rows_ref, d_taps_state_ref
        )
    )
    place_rows_ref[rows:, :] = place_rows_ref[:HEAD_ROWS, :]


def tall(columns, place):
    return pl.BlockSpec((CHUNK, columns), lambda c: (place(c), 0))


def ssd_specs(width, heads, place):
    def wide(count):
        return pl.BlockSpec((count, CHUNK), lambda c: (0, place(c)))

    def fixed(*shape):
        return pl.BlockSpec(shape, lambda c: (0, 0))

    return [
        tall(width, place), tall(2 * NS, place), fixed(KC, width), fixed(KC, 2 * NS),
        fixed(1, width), tall(heads, place), wide(heads), fixed(1, heads), fixed(heads, 1),
        tall(1, place), wide(1), tall(1, place), tall(1, place), tall(1, place),
    ]


def ssd_forward(inner, selected, taps_inner, taps_state, skip, dt, rate, marks, gate_part):
    rows, width = inner.shape
    heads = dt.shape[1]
    steps = rows // CHUNK

    def place(c):
        return c

    return pl.pallas_call(
        ssd_kernel,
        grid=(steps,),
        in_specs=ssd_specs(width, heads, place) + [tall(width, place)],
        out_specs=(
            tall(width, place),
            tall(width, place),
            tall(1, place),
            tall(width, place),
            tall(2 * NS, place),
            pl.BlockSpec((1, NS, width), lambda c: (c, 0, 0)),
        ),
        out_shape=(
            jax.ShapeDtypeStruct((rows, width), jnp.float32),
            jax.ShapeDtypeStruct((rows, width), jnp.float32),
            jax.ShapeDtypeStruct((rows, 1), jnp.float32),
            jax.ShapeDtypeStruct((rows, width), jnp.float32),
            jax.ShapeDtypeStruct((rows, 2 * NS), jnp.float32),
            jax.ShapeDtypeStruct((steps, NS, width), jnp.float32),
        ),
        scratch_shapes=[
            pltpu.VMEM((NS, width), jnp.float32),
            pltpu.VMEM((CHUNK + HEAD_ROWS, width), jnp.float32),
            pltpu.VMEM((CHUNK + HEAD_ROWS, 2 * NS), jnp.float32),
        ],
        compiler_params=pltpu.CompilerParams(vmem_limit_bytes=48 * 1024 * 1024),
    )(
        inner, selected, taps_inner, taps_state, skip, dt, dt.T, rate[None, :], rate[:, None],
        *marks, gate_part,
    )


def ssd_backward(
    inner, selected, taps_inner, taps_state, skip, dt, rate, marks, pre_inner, pre_state, kept, grad
):
    rows, width = inner.shape
    heads = dt.shape[1]
    steps = rows // CHUNK

    def place(c):
        return steps - 1 - c

    def fixed(*shape):
        return pl.BlockSpec(shape, lambda c: (0, 0))

    return pl.pallas_call(
        ssd_back_kernel,
        grid=(steps,),
        in_specs=ssd_specs(width, heads, place)
        + [
            tall(width, place),
            tall(2 * NS, place),
            pl.BlockSpec((1, NS, width), lambda c: (place(c), 0, 0)),
            tall(width, place),
        ],
        out_specs=(
            tall(width, place),
            tall(2 * NS, place),
            tall(heads, place),
            pl.BlockSpec((1, 1, heads), lambda c: (place(c), 0, 0)),
            fixed(KC, width),
            fixed(KC, 2 * NS),
            fixed(1, width),
        ),
        out_shape=(
            jax.ShapeDtypeStruct((rows, width), jnp.bfloat16),
            jax.ShapeDtypeStruct((rows, 2 * NS), jnp.bfloat16),
            jax.ShapeDtypeStruct((rows, heads), jnp.float32),
            jax.ShapeDtypeStruct((steps, 1, heads), jnp.float32),
            jax.ShapeDtypeStruct((KC, width), jnp.float32),
            jax.ShapeDtypeStruct((KC, 2 * NS), jnp.float32),
            jax.ShapeDtypeStruct((1, width), jnp.float32),
        ),
        scratch_shapes=[
            pltpu.VMEM((NS, width), jnp.float32),
            pltpu.VMEM((CHUNK, width), jnp.float32),
            pltpu.VMEM((CHUNK, width), jnp.float32),
            pltpu.VMEM((CHUNK + HEAD_ROWS, width), jnp.float32),
            pltpu.VMEM((CHUNK + HEAD_ROWS, 2 * NS), jnp.float32),
            pltpu.VMEM((CHUNK + HEAD_ROWS, 1), jnp.int32),
        ],
        compiler_params=pltpu.CompilerParams(vmem_limit_bytes=48 * 1024 * 1024),
    )(
        inner, selected, taps_inner, taps_state, skip, dt, dt.T, rate[None, :], rate[:, None],
        *marks, pre_inner, pre_state, kept, grad,
    )


def chunk_marks(segment, places):
    chunks = segment.reshape(-1, CHUNK)
    before = jnp.concatenate([jnp.full((1,), -1, jnp.int32), chunks[:-1, -1]])
    enters = (chunks == before[:, None]).astype(jnp.float32).reshape(-1, 1)
    leaves = (chunks == chunks[:, -1:]).astype(jnp.float32).reshape(-1, 1)
    return segment[:, None], segment[None, :], enters, leaves, places[:, None]


def adam_step(weight_array, gradient_sum, first_moment, second_moment, rate, decay_rate):
    first_new = BETA_ONE * first_moment + (1.0 - BETA_ONE) * gradient_sum
    second_new = BETA_TWO * second_moment + (1.0 - BETA_TWO) * gradient_sum * gradient_sum
    scaled = (
        first_new
        / (1.0 - BETA_ONE**STEP)
        / (jnp.sqrt(second_new / (1.0 - BETA_TWO**STEP)) + ADAM_EPSILON)
    )
    return (first_new, second_new, weight_array - rate * (scaled + decay_rate * weight_array))


BLOCK_CHIPS = 16
AXIS_OF = {8: 0, 4: 1, 2: 2, 1: 3}
ORDERS = {
    1: ((1, 2, 4),),
    2: ((1, 2, 4), (2, 1, 4)),
    3: ((1, 2, 4), (2, 4, 1), (4, 1, 2)),
}


def partner(values):
    return lax.ppermute(values, "tensor", [(0, 1), (1, 0)])


def flip_pairs(bit):
    return [(i, i ^ bit) for i in range(BLOCK_CHIPS)]


def across(values, bit):
    return lax.ppermute(values, "dp", flip_pairs(bit))


def rank_bit(bit):
    return (lax.axis_index("dp") // bit) % 2


def doubled(values, bit):
    other = across(values, bit)
    axis, mine = AXIS_OF[bit], rank_bit(bit)
    shape = values.shape[:axis] + (2,) + values.shape[axis + 1 :]
    both = lax.dynamic_update_slice_in_dim(jnp.zeros(shape, values.dtype), values, mine, axis)
    return lax.dynamic_update_slice_in_dim(both, other, 1 - mine, axis)


def halved(values, bit):
    axis, mine = AXIS_OF[bit], rank_bit(bit)
    keep = lax.dynamic_slice_in_dim(values, mine, 1, axis=axis)
    send = lax.dynamic_slice_in_dim(values, 1 - mine, 1, axis=axis)
    return keep.astype(jnp.float32) + across(send, bit).astype(jnp.float32)


def gather_step(parts, step):
    if lax.axis_size("dp") != BLOCK_CHIPS:
        if step > 0:
            return parts
        return [lax.all_gather(part, "dp", axis=0, tiled=True) for part in parts]
    if step == 0:
        columns = [part.shape[1] for part in parts]
        joined = doubled(jnp.concatenate(parts, axis=1)[None, None, None, None], 8)
        starts = [sum(columns[:g]) for g in range(len(columns))]
        return [joined[..., a : a + n] for a, n in zip(starts, columns)]
    orders = ORDERS[len(parts)]
    parts = [doubled(part, orders[g][3 - step]) for g, part in enumerate(parts)]
    if step < 3:
        return parts
    return [part.reshape(-1, part.shape[-1]) for part in parts]


def gather_rows(shards):
    for step in range(4):
        shards = gather_step(shards, step)
    return shards


def reduce_step(parts, step):
    if lax.axis_size("dp") != BLOCK_CHIPS:
        if step > 0:
            return parts
        joined = jnp.concatenate(parts, axis=1)
        return [
            lax.psum_scatter(joined, "dp", scatter_dimension=0, tiled=True).astype(jnp.float32)
        ]
    if step == 0:
        parts = [part.reshape(2, 2, 2, 2, -1, part.shape[1]) for part in parts]
    if step == 2 and len(parts) == 2:
        parts = [jnp.concatenate(parts, axis=-1)]
    if step < 3:
        orders = ORDERS[len(parts)]
        return [halved(part, orders[g][step]).astype(jnp.bfloat16) for g, part in enumerate(parts)]
    total = halved(jnp.concatenate(parts, axis=-1), 8)
    return [total.reshape(-1, total.shape[-1])]


def reduce_rows(wholes):
    for step in range(4):
        wholes = reduce_step(wholes, step)
    return wholes[0]


def tied(transfer, computed):
    return lax.optimization_barrier((transfer, computed))


def sum_everywhere(values):
    if lax.axis_size("dp") != BLOCK_CHIPS:
        return lax.psum(values, ("dp", "tensor"))
    values = values + partner(values)
    for bit in (1, 2, 4, 8):
        values = values + across(values, bit)
    return values


def in_order(mine, other, tensor_rank):
    return jnp.where(
        tensor_rank == 0,
        jnp.concatenate([mine, other], axis=0),
        jnp.concatenate([other, mine], axis=0),
    )


def split_sum(partial, tensor_rank):
    half = partial.shape[0] // 2
    keep = lax.dynamic_slice_in_dim(partial, tensor_rank * half, half, axis=0)
    send = lax.dynamic_slice_in_dim(partial, (1 - tensor_rank) * half, half, axis=0)
    return keep, partner(send)


def local(
    residual,
    cotangent,
    segment,
    expand,
    expand_first,
    expand_second,
    select,
    select_first,
    select_second,
    attention,
    attention_moment_one,
    attention_moment_two,
    project,
    project_first,
    project_second,
    combine,
    combine_first,
    combine_second,
    widening,
    widening_first,
    widening_second,
    narrowing,
    narrowing_first,
    narrowing_second,
    kernel,
    kernel_first,
    kernel_second,
    scales,
    scales_first,
    scales_second,
    decays,
    decays_first,
    decays_second,
):
    tensor_rank = lax.axis_index("tensor")
    width_local = expand.shape[2]
    heads_local = width_local // PD
    kv_local = attention.shape[1]
    width_ff = widening.shape[2]
    token_positions = token_places(segment)
    gain_first = scales[:MODEL_WIDTH]
    gain_second = scales[MODEL_WIDTH : 2 * MODEL_WIDTH]
    gain_inner = lax.dynamic_slice_in_dim(
        scales, 2 * MODEL_WIDTH + tensor_rank * width_local, width_local
    )
    taps_inner = lax.dynamic_slice_in_dim(kernel, tensor_rank * width_local, width_local, axis=1)
    taps_state = kernel[:, DSSM:]
    rates_local = lax.dynamic_slice_in_dim(decays, tensor_rank * heads_local, heads_local, axis=1)
    resid_float = residual.astype(jnp.float32)
    normed_input, first_back = jax.vjp(rms_apply, resid_float, gain_first)
    normed_low = normed_input.astype(jnp.bfloat16)
    normed_all = in_order(normed_low, partner(normed_low), tensor_rank)
    low = jnp.bfloat16
    rows_local = expand.shape[0]
    gate_weights, inner_weights, attention_weights = gather_rows(
        [
            expand[:, 0].astype(low),
            expand[:, 1].astype(low),
            attention.reshape(rows_local, -1).astype(low),
        ]
    )
    other_weights = lax.all_gather(
        jnp.concatenate(
            [
                project.T.astype(low),
                combine.T.astype(low),
                widening.reshape(rows_local, -1).astype(low),
                narrowing.T.astype(low),
            ],
            axis=1,
        ),
        "dp",
        axis=0,
        tiled=True,
    )
    width_mix = width_local + combine.shape[0]
    mix_out_weights = other_weights[:, :width_mix]
    widening_weights = other_weights[:, width_mix : width_mix + 2 * width_ff]
    narrowing_weights = other_weights[:, width_mix + 2 * width_ff :]
    select_low = select.astype(low)
    selected = product(normed_all, select_low)
    cosine, sine = rotary_tables(token_positions)
    marks = chunk_marks(segment, token_positions)
    seg_col, seg_row = marks[:2]
    log_rates, skip_gains, step_bias = rates_local
    step_raw = lax.dynamic_slice_in_dim(
        selected, 2 * NS + tensor_rank * heads_local, heads_local, axis=1
    )
    step_sizes, step_back = jax.vjp(lambda v, w: jax.nn.softplus(v + w), step_raw, step_bias)
    rates = -jnp.exp(log_rates)
    skip = jnp.repeat(skip_gains, PD)[None, :]
    packed_tokens = product(normed_all, attention_weights)
    attended = attend_forward(packed_tokens, cosine, sine, seg_col, seg_row)
    (inner_weights, gate_weights), attended = tied((inner_weights, gate_weights), attended)
    attended_low, rotated, peaks = attended
    inner = product(normed_all, inner_weights)
    gate_part = product(normed_all, gate_weights)
    ssd_inputs = (inner, selected, taps_inner, taps_state, skip, step_sizes, rates, marks)
    gated, y, squares, pre_inner, pre_state, kept_states = ssd_forward(*ssd_inputs, gate_part)
    square_sum = squares + partner(squares)
    spread_inverse = lax.rsqrt(square_sum / DSSM + EPSILON)
    inner_normed = gated * spread_inverse * gain_inner
    mixed_low = jnp.concatenate([inner_normed.astype(low), attended_low], axis=1)
    mixed_keep, mixed_other = split_sum(product_nt(mixed_low, mix_out_weights), tensor_rank)
    hidden = resid_float + (mixed_keep + mixed_other)
    normed_two, second_back = jax.vjp(rms_apply, hidden, gain_second)
    normed_two_low = normed_two.astype(low)
    normed_two_all = jnp.concatenate([normed_two_low, partner(normed_two_low)], axis=0)
    half_rows = residual.shape[0]
    gate_up = product(normed_two_all, widening_weights)
    gate_values = gate_up[:, :width_ff]
    up_values = gate_up[:, width_ff:]
    sigmoid_gate = jax.nn.sigmoid(gate_values)
    activated = (gate_values * sigmoid_gate * up_values).astype(jnp.bfloat16)
    ffn_part = product_nt(activated, narrowing_weights).astype(jnp.bfloat16)
    ffn_out = ffn_part[:half_rows].astype(jnp.float32) + partner(ffn_part[half_rows:]).astype(
        jnp.float32
    )
    output = (hidden + ffn_out).astype(jnp.bfloat16)
    cot_all = jnp.concatenate([cotangent, partner(cotangent)], axis=0)
    d_activated = product(cot_all, narrowing_weights)
    grad_narrowing = product_tn(cot_all, activated).astype(low)
    d_gate = (
        d_activated * up_values * (sigmoid_gate + gate_values * sigmoid_gate * (1.0 - sigmoid_gate))
    )
    d_up = d_activated * (gate_values * sigmoid_gate)
    d_gate_up = jnp.concatenate([d_gate, d_up], axis=1).astype(low)
    grad_widening = product_tn(normed_two_all, d_gate_up).astype(low)
    d_normed_two_part = product_nt(d_gate_up, widening_weights)
    d_normed_two = d_normed_two_part[:half_rows] + partner(d_normed_two_part[half_rows:])
    d_hidden_norm, grad_gain_second = second_back(d_normed_two)
    d_hidden = cotangent.astype(jnp.float32) + d_hidden_norm
    d_hidden_low = d_hidden.astype(low)
    d_hidden_all = in_order(d_hidden_low, partner(d_hidden_low), tensor_rank)
    ffn_grads, d_hidden_all = tied(
        jnp.concatenate([grad_widening, grad_narrowing], axis=1), d_hidden_all
    )
    ffn_sum = lax.psum_scatter(ffn_grads, "dp", scatter_dimension=0, tiled=True).astype(
        jnp.float32
    )
    d_mix_out = product(d_hidden_all, mix_out_weights)
    d_inner_normed = d_mix_out[:, :width_local]
    d_packed_low = attend_backward(
        rotated, peaks, d_mix_out[:, width_local:], cosine, sine, seg_col, seg_row
    )
    scaled_grad = d_inner_normed * gain_inner
    along = jnp.sum(scaled_grad * gated, axis=1, keepdims=True)
    along = along + partner(along)
    grad_gain_inner = jnp.sum(d_inner_normed * gated * spread_inverse, axis=0)
    d_gated = scaled_grad * spread_inverse - gated * (along * spread_inverse**3 / DSSM)
    sigmoid_part = jax.nn.sigmoid(gate_part)
    d_y = d_gated * (gate_part * sigmoid_part)
    d_gate_low = (
        d_gated * y * (sigmoid_part * (1.0 + gate_part * (1.0 - sigmoid_part)))
    ).astype(low)
    grad_mix_out = product_tn(d_hidden_all, mixed_low).astype(low)
    grad_gate = product_tn(normed_all, d_gate_low).astype(low)
    grad_attention = product_tn(normed_all, d_packed_low).astype(low)
    early_parts = [grad_mix_out, jnp.concatenate([grad_gate, grad_attention], axis=1)]
    early_parts, d_y = tied(early_parts, d_y)
    early_parts = reduce_step(early_parts, 0)
    ssd_grads = ssd_backward(*ssd_inputs, pre_inner, pre_state, kept_states, d_y)
    early_parts, ssd_grads = tied(early_parts, ssd_grads)
    early_parts = reduce_step(early_parts, 1)
    d_inner_low, d_state_low, d_step_sizes, d_rates, grad_taps_inner, grad_taps_state, d_skip = (
        ssd_grads
    )
    d_step_raw, d_bias = step_back(d_step_sizes)
    grad_rates = jnp.stack(
        [
            jnp.sum(d_rates, axis=(0, 1)) * rates,
            jnp.sum(d_skip.reshape(heads_local, PD), axis=1),
            d_bias,
        ]
    )
    d_steps_low = lax.dynamic_update_slice_in_dim(
        jnp.zeros((segment.shape[0], selected.shape[1] - 2 * NS), low),
        d_step_raw.astype(low),
        tensor_rank * heads_local,
        axis=1,
    )
    d_selected_low = jnp.concatenate([d_state_low, d_steps_low], axis=1)
    grad_select = product_tn(normed_all, d_selected_low)
    grad_inner = product_tn(normed_all, d_inner_low).astype(low)
    kernel_grad = lax.dynamic_update_slice_in_dim(
        jnp.zeros_like(kernel), grad_taps_inner, tensor_rank * width_local, axis=1
    )
    kernel_grad = lax.dynamic_update_slice_in_dim(kernel_grad, grad_taps_state, DSSM, axis=1)
    decays_grad = lax.dynamic_update_slice_in_dim(
        jnp.zeros_like(decays), grad_rates, tensor_rank * heads_local, axis=1
    )
    inner_gain_grad = lax.dynamic_update_slice_in_dim(
        jnp.zeros((DSSM,), jnp.float32), grad_gain_inner, tensor_rank * width_local, axis=0
    )
    small = jnp.concatenate(
        [kernel_grad.reshape(-1), grad_gain_second, inner_gain_grad, decays_grad.reshape(-1)]
    )
    small_size = small.shape[0]
    small_columns = -(-small_size // MODEL_WIDTH)
    small = jnp.pad(small, (0, small_columns * MODEL_WIDTH - small_size))
    select_columns = select.shape[1]
    shared = jnp.concatenate(
        [grad_select, small.reshape(MODEL_WIDTH, small_columns)], axis=1
    ).astype(low)
    shared = jnp.pad(shared, ((0, 0), (0, -shared.shape[1] % 128)))
    (shared, grad_inner), d_inner_low = tied((shared, grad_inner), d_inner_low)
    shared_rows = reduce_rows([shared])
    shared = gather_rows([shared_rows + partner(shared_rows)])[0]
    select_total = shared[:, :select_columns]
    small = shared[:, select_columns : select_columns + small_columns].reshape(-1)
    d_normed_part = (
        product_nt(d_gate_low, gate_weights)
        + product_nt(d_packed_low, attention_weights)
        + product_nt(d_inner_low, inner_weights)
        + product_nt(d_selected_low, select_low)
    ).astype(low)
    d_normed_keep, d_normed_other = split_sum(d_normed_part, tensor_rank)
    d_normed = d_normed_keep.astype(jnp.float32) + d_normed_other.astype(jnp.float32)
    d_resid_norm, grad_gain_first = first_back(d_normed)
    gradient = d_hidden + d_resid_norm
    gain_first_total = sum_everywhere(grad_gain_first)
    inner_sum = reduce_rows([grad_inner])
    early_sum = reduce_step(reduce_step(early_parts, 2), 3)[0]
    widening_sum = ffn_sum[:, : 2 * width_ff]
    narrowing_sum = ffn_sum[:, 2 * width_ff :]
    mix_out_sum = early_sum[:, : grad_mix_out.shape[1]]
    gate_sum = early_sum[:, grad_mix_out.shape[1] : grad_mix_out.shape[1] + width_local]
    attention_sum = early_sum[:, grad_mix_out.shape[1] + width_local :]
    large_grads = (
        jnp.stack([gate_sum, inner_sum], axis=1),
        attention_sum.reshape(attention.shape),
        widening_sum.reshape(widening.shape),
        mix_out_sum[:, :width_local].T,
        mix_out_sum[:, width_local:].T,
        narrowing_sum.T,
    )
    kernel_size = kernel.size
    kernel_total = small[:kernel_size].reshape(kernel.shape)
    rest = scales.shape[0] - MODEL_WIDTH
    scales_total = jnp.concatenate([gain_first_total, small[kernel_size : kernel_size + rest]])
    decays_total = small[kernel_size + rest : small_size].reshape(decays.shape)
    expand_mean, expand_square, expand_update = adam_step(
        expand, large_grads[0], expand_first, expand_second, RATE_MATRIX, WEIGHT_DECAY
    )
    select_mean, select_square, select_update = adam_step(
        select, select_total, select_first, select_second, RATE_MATRIX, WEIGHT_DECAY
    )
    attention_mean, attention_square, attention_update = adam_step(
        attention,
        large_grads[1],
        attention_moment_one,
        attention_moment_two,
        RATE_MATRIX,
        WEIGHT_DECAY,
    )
    project_mean, project_square, project_update = adam_step(
        project, large_grads[3], project_first, project_second, RATE_PROJECT, WEIGHT_DECAY
    )
    combine_mean, combine_square, combine_update = adam_step(
        combine, large_grads[4], combine_first, combine_second, RATE_COMBINE, WEIGHT_DECAY
    )
    widening_mean, widening_square, widening_update = adam_step(
        widening, large_grads[2], widening_first, widening_second, RATE_MATRIX, WEIGHT_DECAY
    )
    narrowing_mean, narrowing_square, narrowing_update = adam_step(
        narrowing, large_grads[5], narrowing_first, narrowing_second, RATE_NARROWING, WEIGHT_DECAY
    )
    kernel_mean, kernel_square, kernel_update = adam_step(
        kernel, kernel_total, kernel_first, kernel_second, RATE_KERNEL, 0.0
    )
    scales_mean, scales_square, scales_update = adam_step(
        scales, scales_total, scales_first, scales_second, RATE_SCALES, 0.0
    )
    decays_mean, decays_square, decays_update = adam_step(
        decays, decays_total, decays_first, decays_second, RATE_DECAYS, 0.0
    )
    return (
        output,
        gradient,
        expand_mean,
        expand_square,
        expand_update,
        select_mean,
        select_square,
        select_update,
        attention_mean,
        attention_square,
        attention_update,
        project_mean,
        project_square,
        project_update,
        combine_mean,
        combine_square,
        combine_update,
        widening_mean,
        widening_square,
        widening_update,
        narrowing_mean,
        narrowing_square,
        narrowing_update,
        kernel_mean,
        kernel_square,
        kernel_update,
        scales_mean,
        scales_square,
        scales_update,
        decays_mean,
        decays_square,
        decays_update,
    )


def solution(mesh):
    placed = (
        P(("dp", "tensor"), None),
        P(("dp", "tensor"), None),
        P("dp"),
        P("dp", None, "tensor"),
        P("dp", None, "tensor"),
        P("dp", None, "tensor"),
        P(),
        P(),
        P(),
        P("dp", "tensor", None),
        P("dp", "tensor", None),
        P("dp", "tensor", None),
        P("tensor", "dp"),
        P("tensor", "dp"),
        P("tensor", "dp"),
        P("tensor", "dp"),
        P("tensor", "dp"),
        P("tensor", "dp"),
        P("dp", None, "tensor"),
        P("dp", None, "tensor"),
        P("dp", None, "tensor"),
        P("tensor", "dp"),
        P("tensor", "dp"),
        P("tensor", "dp"),
        P(),
        P(),
        P(),
        P(),
        P(),
        P(),
        P(),
        P(),
        P(),
    )
    return jax.shard_map(
        local,
        mesh=mesh,
        in_specs=placed,
        out_specs=(
            P(("dp", "tensor"), None),
            P(("dp", "tensor"), None),
            P("dp", None, "tensor"),
            P("dp", None, "tensor"),
            P("dp", None, "tensor"),
            P(),
            P(),
            P(),
            P("dp", "tensor", None),
            P("dp", "tensor", None),
            P("dp", "tensor", None),
            P("tensor", "dp"),
            P("tensor", "dp"),
            P("tensor", "dp"),
            P("tensor", "dp"),
            P("tensor", "dp"),
            P("tensor", "dp"),
            P("dp", None, "tensor"),
            P("dp", None, "tensor"),
            P("dp", None, "tensor"),
            P("tensor", "dp"),
            P("tensor", "dp"),
            P("tensor", "dp"),
            P(),
            P(),
            P(),
            P(),
            P(),
            P(),
            P(),
            P(),
            P(),
        ),
        check_vma=False,
    )
```

```python
import math

import jax
import jax.numpy as jnp
from jax import lax
from jax.experimental import pallas as pl
from jax.experimental.pallas import tpu as pltpu
from jax.sharding import PartitionSpec as P

MODEL_WIDTH = 1024
PD = 64
NS = 128
HD = 64
STEP = 10
DSSM = 1536
GROUP_COLUMNS = 384
KC = 4


EPSILON = 1e-05
ROPE_BASE = 10000.0
MASKED = -1e30
BETA_ONE = 0.9
BETA_TWO = 0.95
ADAM_EPSILON = 1e-08
WEIGHT_DECAY = 0.1
RATE_MATRIX = 0.1
RATE_PROJECT = 0.08
RATE_COMBINE = 0.5
RATE_NARROWING = 0.07
RATE_KERNEL = 1.0
RATE_SCALES = 0.5
RATE_DECAYS = 1.0


def product(left_side, right_side):
    return jnp.dot(left_side, right_side, preferred_element_type=jnp.float32)


def product_nt(left_side, right_side):
    return lax.dot_general(
        left_side, right_side, (((1,), (1,)), ((), ())), preferred_element_type=jnp.float32
    )


def product_tn(left_side, right_side):
    return lax.dot_general(
        left_side, right_side, (((0,), (0,)), ((), ())), preferred_element_type=jnp.float32
    )


def sigmoid_linear(values):
    return values * jax.nn.sigmoid(values)


def rms_apply(values, gain_vector):
    return (
        values
        * lax.rsqrt(jnp.mean(values * values, axis=-1, keepdims=True) + EPSILON)
        * gain_vector
    )


def token_places(segment):
    row_count = segment.shape[0]
    row_index = jnp.arange(row_count, dtype=jnp.int32)
    seq_edges = jnp.concatenate([jnp.ones((1,), bool), segment[1:] != segment[:-1]])
    seq_starts = lax.cummax(jnp.where(seq_edges, row_index, 0), axis=0)
    return row_index - seq_starts


CHUNK = 256
HEAD_ROWS = 8


def dot_nn(a, b):
    return jnp.dot(a, b, preferred_element_type=jnp.float32)


def dot_nt(a, b):
    return lax.dot_general(a, b, (((1,), (1,)), ((), ())), preferred_element_type=jnp.float32)


def dot_tn(a, b):
    return lax.dot_general(a, b, (((0,), (0,)), ((), ())), preferred_element_type=jnp.float32)


def low_of(values):
    return values.astype(jnp.bfloat16)


def two_of(values):
    high = values.astype(jnp.bfloat16)
    return high, (values - high.astype(jnp.float32)).astype(jnp.bfloat16)


def fine(dot, a, b):
    a_high, a_low = two_of(a)
    b_high, b_low = two_of(b)
    return dot(a_high, b_high) + (dot(a_high, b_low) + dot(a_low, b_high))


def fine_left(dot, a, exact):
    a_high, a_low = two_of(a)
    return dot(a_high, exact) + dot(a_low, exact)


def fine_right(dot, exact, b):
    b_high, b_low = two_of(b)
    b_rest = b - b_high.astype(jnp.float32) - b_low.astype(jnp.float32)
    return dot(exact, b_high) + (dot(exact, b_low) + dot(exact, b_rest.astype(jnp.bfloat16)))


def allowed_pairs(seg_col, seg_row, row_start):
    rows, columns = seg_col.shape[0], seg_row.shape[1]
    row_index = lax.broadcasted_iota(jnp.int32, (rows, columns), 0) + row_start
    column_index = lax.broadcasted_iota(jnp.int32, (rows, columns), 1)
    return (seg_col == seg_row) & (row_index >= column_index)


def swap_halves(values):
    width = values.shape[1]
    lane = lax.broadcasted_iota(jnp.int32, values.shape, 1)
    after = pltpu.roll(values, width - HD // 2, 1)
    before = pltpu.roll(values, HD // 2, 1)
    return jnp.where(lane % HD < HD // 2, after, before)


def turn_parts(cosine_ref, sine_ref, heads):
    scale = 1.0 / math.sqrt(HD)
    cosine, sine = cosine_ref[...], sine_ref[...]
    is_key = lax.broadcasted_iota(jnp.int32, cosine.shape, 1) < HD
    for h in range(0, heads, 2):
        yield slice(h * HD, (h + 2) * HD), cosine * scale, sine * scale
    yield (
        slice(heads * HD, (heads + 2) * HD),
        jnp.where(is_key, cosine, 1.0),
        jnp.where(is_key, sine, 0.0),
    )


def attend_kernel(packed_ref, cosine_ref, sine_ref, col_ref, row_ref, out_ref, rotated_ref, peak_ref):
    heads = out_ref.shape[1] // HD
    for at, cosine, sine in turn_parts(cosine_ref, sine_ref, heads):
        values = packed_ref[:, at]
        rotated_ref[:, at] = low_of(values * cosine + swap_halves(values) * sine)
    for start in range(0, out_ref.shape[0], CHUNK):
        stop = start + CHUNK
        mask = allowed_pairs(col_ref[start:stop, :], row_ref[:, :stop], start)
        keys = rotated_ref[:stop, heads * HD : (heads + 1) * HD]
        value_rows = rotated_ref[:stop, (heads + 1) * HD :]
        for h in range(heads):
            query = rotated_ref[start:stop, h * HD : (h + 1) * HD]
            scores = jnp.where(mask, dot_nt(query, keys), MASKED)
            peak = jnp.max(scores, axis=1, keepdims=True)
            weights = jnp.exp(scores - peak)
            total = jnp.sum(weights, axis=1, keepdims=True)
            out_ref[start:stop, h * HD : (h + 1) * HD] = low_of(
                dot_nn(low_of(weights), value_rows) / total
            )
            peak_ref[start:stop, h : h + 1] = peak + jnp.log(total)


def attend_back_kernel(
    rotated_ref, peak_ref, grad_ref, cosine_ref, sine_ref, col_ref, row_ref, out_ref, acc_ref
):
    heads = grad_ref.shape[1] // HD
    at_key, at_value = heads * HD, (heads + 1) * HD
    acc_ref[:, at_key:] = jnp.zeros((acc_ref.shape[0], 2 * HD), jnp.float32)
    for start in range(0, grad_ref.shape[0], CHUNK):
        stop = start + CHUNK
        mask = allowed_pairs(col_ref[start:stop, :], row_ref[:, :stop], start)
        keys = rotated_ref[:stop, at_key:at_value]
        value_rows = rotated_ref[:stop, at_value:]
        d_keys = jnp.zeros((stop, HD), jnp.float32)
        d_values = jnp.zeros((stop, HD), jnp.float32)
        for h in range(heads):
            query = rotated_ref[start:stop, h * HD : (h + 1) * HD]
            grad = low_of(grad_ref[start:stop, h * HD : (h + 1) * HD])
            scores = jnp.where(mask, dot_nt(query, keys), MASKED)
            weights = jnp.exp(scores - peak_ref[start:stop, h : h + 1])
            d_weights = dot_nt(grad, value_rows)
            mean = jnp.sum(weights * d_weights, axis=1, keepdims=True)
            d_scores = low_of(weights * (d_weights - mean))
            acc_ref[start:stop, h * HD : (h + 1) * HD] = dot_nn(d_scores, keys)
            d_keys = d_keys + dot_tn(d_scores, query)
            d_values = d_values + dot_tn(low_of(weights), grad)
        acc_ref[:stop, at_key:at_value] += d_keys
        acc_ref[:stop, at_value:] += d_values
    for at, cosine, sine in turn_parts(cosine_ref, sine_ref, heads):
        grads = acc_ref[:, at]
        out_ref[:, at] = low_of(grads * cosine + swap_halves(grads * sine))


def whole_call(kernel, out_shape, scratch_shapes=()):
    return pl.pallas_call(
        kernel,
        out_shape=out_shape,
        scratch_shapes=list(scratch_shapes),
        compiler_params=pltpu.CompilerParams(vmem_limit_bytes=48 * 1024 * 1024),
    )


def attend_forward(packed, cosine, sine, seg_col, seg_row):
    rows, columns = packed.shape
    heads = columns // HD - 2
    return whole_call(
        attend_kernel,
        (
            jax.ShapeDtypeStruct((rows, heads * HD), jnp.bfloat16),
            jax.ShapeDtypeStruct((rows, columns), jnp.bfloat16),
            jax.ShapeDtypeStruct((rows, heads), jnp.float32),
        ),
    )(packed, cosine, sine, seg_col, seg_row)


def attend_backward(rotated, peaks, grad, cosine, sine, seg_col, seg_row):
    rows, columns = rotated.shape
    return whole_call(
        attend_back_kernel,
        jax.ShapeDtypeStruct((rows, columns), jnp.bfloat16),
        [pltpu.VMEM((rows, columns), jnp.float32)],
    )(rotated, peaks, grad, cosine, sine, seg_col, seg_row)


def rotary_tables(places):
    halfsize = HD // 2
    lane = jnp.arange(2 * HD, dtype=jnp.int32) % HD
    frequency = ROPE_BASE ** (-(lane % halfsize).astype(jnp.float32) * 2.0 / HD)
    angles = places.astype(jnp.float32)[:, None] * frequency[None, :]
    return jnp.cos(angles), jnp.where(lane < halfsize, -1.0, 1.0)[None, :] * jnp.sin(angles)


def spread_matrix(heads):
    row = lax.broadcasted_iota(jnp.int32, (heads, heads * PD), 0)
    column = lax.broadcasted_iota(jnp.int32, (heads, heads * PD), 1)
    return jnp.where(column // PD == row, 1.0, 0.0).astype(jnp.bfloat16)


def spread_row(values, spread):
    return fine_left(dot_nn, jnp.broadcast_to(values, (8, values.shape[1])), spread)[:1]


def chunk_decays(dt_ref, dt_row_ref, rate_ref, rate_row_ref, in_ref, out_ref):
    rows = dt_ref.shape[0]
    row = lax.broadcasted_iota(jnp.int32, (rows, rows), 0)
    column = lax.broadcasted_iota(jnp.int32, (rows, rows), 1)
    lower = jnp.where(row >= column, 1.0, 0.0).astype(jnp.bfloat16)
    dt = dt_ref[...]
    running = fine_right(dot_nn, lower, dt * rate_ref[...])
    rate_rows = dt_row_ref[...] * rate_row_ref[...]
    high, mid = two_of(rate_rows)
    rest = low_of(rate_rows - high.astype(jnp.float32) - mid.astype(jnp.float32))
    running_row = dot_nt(high, lower) + (dot_nt(mid, lower) + dot_nt(rest, lower))
    last = running[rows - 1 :, :]
    entering = jnp.exp(running) * in_ref[...]
    leaving = jnp.exp(last - running) * out_ref[...]
    keep = jnp.exp(last) * in_ref[rows - 1 :, :]
    return lower, dt, running, running_row, entering, leaving, keep


def filtered(rows_ref, values, taps_ref, places):
    rows = values.shape[0]
    rows_ref[HEAD_ROWS:, :] = values
    summed = taps_ref[0:1, :] * values
    for k in range(1, taps_ref.shape[0]):
        shifted = rows_ref[HEAD_ROWS - k : HEAD_ROWS - k + rows, :]
        summed = summed + taps_ref[k : k + 1, :] * jnp.where(places >= k, shifted, 0.0)
    rows_ref[:HEAD_ROWS, :] = rows_ref[rows:, :]
    return summed


def filter_back(rows_ref, values, grad, taps_ref, places_ref, d_taps_ref):
    rows = values.shape[0]
    rows_ref[:rows, :] = grad
    d_taps_ref[0:1, :] += jnp.sum(values * grad, axis=0, keepdims=True)
    d_values = taps_ref[0:1, :] * grad
    for k in range(1, taps_ref.shape[0]):
        shifted = jnp.where(places_ref[k : k + rows, :] >= k, rows_ref[k : k + rows, :], 0.0)
        d_values = d_values + taps_ref[k : k + 1, :] * shifted
        d_taps_ref[k : k + 1, :] += jnp.sum(values * shifted, axis=0, keepdims=True)
    rows_ref[rows:, :] = rows_ref[:HEAD_ROWS, :]
    return d_values


def slope(values):
    sigmoid = jax.nn.sigmoid(values)
    return sigmoid * (1.0 + values * (1.0 - sigmoid))


def ssd_kernel(
    inner_ref, raw_ref, taps_inner_ref, taps_state_ref, skip_ref,
    dt_ref, dt_row_ref, rate_ref, rate_row_ref, col_ref, row_ref, in_ref, out_mask_ref, places_ref,
    gate_ref,
    gated_ref, y_ref, squares_ref, pre_inner_ref, pre_state_ref, kept_ref,
    state_ref, inner_rows_ref, state_rows_ref,
):
    @pl.when(pl.program_id(0) == 0)
    def _():
        state_ref[...] = jnp.zeros_like(state_ref)
        inner_rows_ref[:HEAD_ROWS, :] = jnp.zeros((HEAD_ROWS, inner_rows_ref.shape[1]), jnp.float32)
        state_rows_ref[:HEAD_ROWS, :] = jnp.zeros((HEAD_ROWS, state_rows_ref.shape[1]), jnp.float32)

    heads = dt_ref.shape[1]
    spread = spread_matrix(heads)
    _, dt, running, running_row, entering, leaving, keep = chunk_decays(
        dt_ref, dt_row_ref, rate_ref, rate_row_ref, in_ref, out_mask_ref
    )
    places = places_ref[...]
    pre_inner = filtered(inner_rows_ref, inner_ref[...], taps_inner_ref, places)
    pre_state = filtered(state_rows_ref, raw_ref[...], taps_state_ref, places)
    pre_inner_ref[...] = pre_inner
    pre_state_ref[...] = pre_state
    mixed = sigmoid_linear(pre_inner)
    states = sigmoid_linear(pre_state)
    inputs_b, readout = states[:, :NS], states[:, NS:]
    mask = allowed_pairs(col_ref[...], row_ref[...], 0)
    scaled = mixed * fine_left(dot_nn, dt, spread)
    scaled_low = low_of(scaled)
    coupling = jnp.where(mask, fine(dot_nt, readout, inputs_b), 0.0)
    state = state_ref[...]
    kept_ref[0] = state
    y_ref[...] = skip_ref[...] * mixed + fine(dot_nn, readout, state) * fine_left(
        dot_nn, entering, spread
    )
    for h in range(heads):
        gap = jnp.where(mask, running[:, h : h + 1] - running_row[h : h + 1, :], MASKED)
        weights = low_of(coupling * jnp.exp(gap))
        y_ref[:, h * PD : (h + 1) * PD] += dot_nn(weights, scaled_low[:, h * PD : (h + 1) * PD])
    gated = y_ref[...] * sigmoid_linear(gate_ref[...])
    gated_ref[...] = gated
    squares_ref[...] = jnp.sum(gated * gated, axis=1, keepdims=True)
    state_ref[...] = state * spread_row(keep, spread) + fine(
        dot_tn, inputs_b, scaled * fine_left(dot_nn, leaving, spread)
    )


def ssd_back_kernel(
    inner_ref, raw_ref, taps_inner_ref, taps_state_ref, skip_ref,
    dt_ref, dt_row_ref, rate_ref, rate_row_ref, col_ref, row_ref, in_ref, out_mask_ref, places_ref,
    pre_inner_ref, pre_state_ref, kept_ref, grad_ref,
    d_inner_ref, d_raw_ref, d_dt_ref, d_rate_ref, d_taps_inner_ref, d_taps_state_ref, d_skip_ref,
    carry_ref, within_ref, d_scaled_ref, inner_rows_ref, state_rows_ref, place_rows_ref,
):
    rows, heads = dt_ref.shape

    @pl.when(pl.program_id(0) == 0)
    def _():
        carry_ref[...] = jnp.zeros_like(carry_ref)
        d_taps_inner_ref[...] = jnp.zeros_like(d_taps_inner_ref)
        d_taps_state_ref[...] = jnp.zeros_like(d_taps_state_ref)
        d_skip_ref[...] = jnp.zeros_like(d_skip_ref)
        inner_rows_ref[rows:, :] = jnp.zeros((HEAD_ROWS, inner_rows_ref.shape[1]), jnp.float32)
        state_rows_ref[rows:, :] = jnp.zeros((HEAD_ROWS, state_rows_ref.shape[1]), jnp.float32)
        place_rows_ref[rows:, :] = jnp.zeros((HEAD_ROWS, 1), jnp.int32)

    spread = spread_matrix(heads)
    lower, dt, running, running_row, entering, leaving, keep = chunk_decays(
        dt_ref, dt_row_ref, rate_ref, rate_row_ref, in_ref, out_mask_ref
    )
    mask = allowed_pairs(col_ref[...], row_ref[...], 0)
    pre_inner, pre_state = pre_inner_ref[...], pre_state_ref[...]
    mixed = sigmoid_linear(pre_inner)
    states = sigmoid_linear(pre_state)
    inputs_b, readout = states[:, :NS], states[:, NS:]
    dt_spread = fine_left(dot_nn, dt, spread)
    scaled = mixed * dt_spread
    scaled_low = low_of(scaled)
    grad = grad_ref[...]
    grad_low = low_of(grad)
    coupling = jnp.where(mask, fine(dot_nt, readout, inputs_b), 0.0)
    d_coupling = jnp.zeros_like(coupling)
    for h in range(heads):
        at = slice(h * PD, (h + 1) * PD)
        gap = jnp.where(mask, running[:, h : h + 1] - running_row[h : h + 1, :], MASKED)
        decay = jnp.exp(gap)
        weights = low_of(coupling * decay)
        d_coupling = d_coupling + dot_nt(grad_low[:, at], scaled_low[:, at]) * decay
        d_scaled_ref[:, at] = dot_tn(weights, grad_low[:, at])
        within_ref[:, at] = dot_nn(weights, scaled_low[:, at])
    state = kept_ref[0]
    carry = carry_ref[...]
    entering_spread = fine_left(dot_nn, entering, spread)
    leaving_spread = fine_left(dot_nn, leaving, spread)
    keep_spread = spread_row(keep, spread)
    grad_in = grad * entering_spread
    scaled_out = scaled * leaving_spread
    from_state = fine(dot_nn, readout, state) * grad_in
    d_scaled_state = fine(dot_nn, inputs_b, carry) * leaving_spread
    to_state = scaled * d_scaled_state
    d_scaled_within = d_scaled_ref[...]
    own = grad_low.astype(jnp.float32) * within_ref[...]
    own = own - scaled_low.astype(jnp.float32) * d_scaled_within
    d_running = fine_left(dot_nt, own + from_state - to_state, spread)
    at_end = jnp.sum(to_state, axis=0, keepdims=True) + keep_spread * jnp.sum(
        carry * state, axis=0, keepdims=True
    )
    at_end = fine_left(dot_nt, jnp.broadcast_to(at_end, (8, at_end.shape[1])), spread)[:1]
    d_high, d_rest = two_of(d_running)
    d_rate = dot_tn(lower, d_high) + dot_tn(lower, d_rest) + at_end
    d_scaled = d_scaled_within + d_scaled_state
    d_dt_ref[...] = fine_left(dot_nt, d_scaled * mixed, spread) + d_rate * rate_ref[...]
    d_rate_ref[0] = jnp.sum(d_rate * dt, axis=0, keepdims=True)
    d_skip_ref[...] += jnp.sum(grad * mixed, axis=0, keepdims=True)
    d_mixed = d_scaled * dt_spread + skip_ref[...] * grad
    d_inputs = fine(dot_tn, d_coupling, readout) + fine(dot_nt, scaled_out, carry)
    d_readout = fine(dot_nn, d_coupling, inputs_b) + fine(dot_nt, grad_in, state)
    carry_ref[...] = carry * keep_spread + fine(dot_tn, readout, grad_in)
    place_rows_ref[:rows, :] = places_ref[...]
    d_inner_ref[...] = low_of(
        filter_back(
            inner_rows_ref, inner_ref[...], d_mixed * slope(pre_inner), taps_inner_ref,
            place_rows_ref, d_taps_inner_ref,
        )
    )
    d_states = jnp.concatenate([d_inputs, d_readout], axis=1) * slope(pre_state)
    d_raw_ref[...] = low_of(
        filter_back(
            state_rows_ref, raw_ref[...], d_states, taps_state_ref, place_rows_ref, d_taps_state_ref
        )
    )
    place_rows_ref[rows:, :] = place_rows_ref[:HEAD_ROWS, :]


def tall(columns, place):
    return pl.BlockSpec((CHUNK, columns), lambda c: (place(c), 0))


def ssd_specs(width, heads, place):
    def wide(count):
        return pl.BlockSpec((count, CHUNK), lambda c: (0, place(c)))

    def fixed(*shape):
        return pl.BlockSpec(shape, lambda c: (0, 0))

    return [
        tall(width, place), tall(2 * NS, place), fixed(KC, width), fixed(KC, 2 * NS),
        fixed(1, width), tall(heads, place), wide(heads), fixed(1, heads), fixed(heads, 1),
        tall(1, place), wide(1), tall(1, place), tall(1, place), tall(1, place),
    ]


def ssd_forward(inner, selected, taps_inner, taps_state, skip, dt, rate, marks, gate_part):
    rows, width = inner.shape
    heads = dt.shape[1]
    steps = rows // CHUNK

    def place(c):
        return c

    return pl.pallas_call(
        ssd_kernel,
        grid=(steps,),
        in_specs=ssd_specs(width, heads, place) + [tall(width, place)],
        out_specs=(
            tall(width, place),
            tall(width, place),
            tall(1, place),
            tall(width, place),
            tall(2 * NS, place),
            pl.BlockSpec((1, NS, width), lambda c: (c, 0, 0)),
        ),
        out_shape=(
            jax.ShapeDtypeStruct((rows, width), jnp.float32),
            jax.ShapeDtypeStruct((rows, width), jnp.float32),
            jax.ShapeDtypeStruct((rows, 1), jnp.float32),
            jax.ShapeDtypeStruct((rows, width), jnp.float32),
            jax.ShapeDtypeStruct((rows, 2 * NS), jnp.float32),
            jax.ShapeDtypeStruct((steps, NS, width), jnp.float32),
        ),
        scratch_shapes=[
            pltpu.VMEM((NS, width), jnp.float32),
            pltpu.VMEM((CHUNK + HEAD_ROWS, width), jnp.float32),
            pltpu.VMEM((CHUNK + HEAD_ROWS, 2 * NS), jnp.float32),
        ],
        compiler_params=pltpu.CompilerParams(vmem_limit_bytes=48 * 1024 * 1024),
    )(
        inner, selected, taps_inner, taps_state, skip, dt, dt.T, rate[None, :], rate[:, None],
        *marks, gate_part,
    )


def ssd_backward(
    inner, selected, taps_inner, taps_state, skip, dt, rate, marks, pre_inner, pre_state, kept, grad
):
    rows, width = inner.shape
    heads = dt.shape[1]
    steps = rows // CHUNK

    def place(c):
        return steps - 1 - c

    def fixed(*shape):
        return pl.BlockSpec(shape, lambda c: (0, 0))

    return pl.pallas_call(
        ssd_back_kernel,
        grid=(steps,),
        in_specs=ssd_specs(width, heads, place)
        + [
            tall(width, place),
            tall(2 * NS, place),
            pl.BlockSpec((1, NS, width), lambda c: (place(c), 0, 0)),
            tall(width, place),
        ],
        out_specs=(
            tall(width, place),
            tall(2 * NS, place),
            tall(heads, place),
            pl.BlockSpec((1, 1, heads), lambda c: (place(c), 0, 0)),
            fixed(KC, width),
            fixed(KC, 2 * NS),
            fixed(1, width),
        ),
        out_shape=(
            jax.ShapeDtypeStruct((rows, width), jnp.bfloat16),
            jax.ShapeDtypeStruct((rows, 2 * NS), jnp.bfloat16),
            jax.ShapeDtypeStruct((rows, heads), jnp.float32),
            jax.ShapeDtypeStruct((steps, 1, heads), jnp.float32),
            jax.ShapeDtypeStruct((KC, width), jnp.float32),
            jax.ShapeDtypeStruct((KC, 2 * NS), jnp.float32),
            jax.ShapeDtypeStruct((1, width), jnp.float32),
        ),
        scratch_shapes=[
            pltpu.VMEM((NS, width), jnp.float32),
            pltpu.VMEM((CHUNK, width), jnp.float32),
            pltpu.VMEM((CHUNK, width), jnp.float32),
            pltpu.VMEM((CHUNK + HEAD_ROWS, width), jnp.float32),
            pltpu.VMEM((CHUNK + HEAD_ROWS, 2 * NS), jnp.float32),
            pltpu.VMEM((CHUNK + HEAD_ROWS, 1), jnp.int32),
        ],
        compiler_params=pltpu.CompilerParams(vmem_limit_bytes=48 * 1024 * 1024),
    )(
        inner, selected, taps_inner, taps_state, skip, dt, dt.T, rate[None, :], rate[:, None],
        *marks, pre_inner, pre_state, kept, grad,
    )


def chunk_marks(segment, places):
    chunks = segment.reshape(-1, CHUNK)
    before = jnp.concatenate([jnp.full((1,), -1, jnp.int32), chunks[:-1, -1]])
    enters = (chunks == before[:, None]).astype(jnp.float32).reshape(-1, 1)
    leaves = (chunks == chunks[:, -1:]).astype(jnp.float32).reshape(-1, 1)
    return segment[:, None], segment[None, :], enters, leaves, places[:, None]


def adam_step(weight_array, gradient_sum, first_moment, second_moment, rate, decay_rate):
    first_new = BETA_ONE * first_moment + (1.0 - BETA_ONE) * gradient_sum
    second_new = BETA_TWO * second_moment + (1.0 - BETA_TWO) * gradient_sum * gradient_sum
    scaled = (
        first_new
        / (1.0 - BETA_ONE**STEP)
        / (jnp.sqrt(second_new / (1.0 - BETA_TWO**STEP)) + ADAM_EPSILON)
    )
    return (first_new, second_new, weight_array - rate * (scaled + decay_rate * weight_array))


BLOCK_CHIPS = 16
AXIS_OF = {8: 0, 4: 1, 2: 2, 1: 3}
ORDERS = {
    1: ((4, 1, 2),),
    2: ((1, 2, 4), (2, 1, 4)),
    3: ((1, 2, 4), (2, 4, 1), (4, 1, 2)),
}


def partner(values):
    return lax.ppermute(values, "tensor", [(0, 1), (1, 0)])


def flip_pairs(bit):
    return [(i, i ^ bit) for i in range(BLOCK_CHIPS)]


def across(values, bit):
    return lax.ppermute(values, "dp", flip_pairs(bit))


def rank_bit(bit):
    return (lax.axis_index("dp") // bit) % 2


def doubled(values, bit):
    return joined(values, across(values, bit), bit)


def joined(values, other, bit):
    axis, mine = AXIS_OF[bit], rank_bit(bit)
    shape = values.shape[:axis] + (2,) + values.shape[axis + 1 :]
    both = lax.dynamic_update_slice_in_dim(jnp.zeros(shape, values.dtype), values, mine, axis)
    return lax.dynamic_update_slice_in_dim(both, other, 1 - mine, axis)


def gather_step(parts, step):
    if lax.axis_size("dp") != BLOCK_CHIPS:
        if step > 0:
            return parts
        return [lax.all_gather(part, "dp", axis=0, tiled=True) for part in parts]
    if step == 0:
        columns = [part.shape[1] for part in parts]
        joined = doubled(jnp.concatenate(parts, axis=1)[None, None, None, None], 8)
        starts = [sum(columns[:g]) for g in range(len(columns))]
        return [joined[..., a : a + n] for a, n in zip(starts, columns)]
    orders = ORDERS[len(parts)]
    parts = [doubled(part, orders[g][3 - step]) for g, part in enumerate(parts)]
    if step < 3:
        return parts
    return [part.reshape(-1, part.shape[-1]) for part in parts]


FLIPS = (1, 2, 3)


def spread_send(part, step):
    if lax.axis_size("dp") != BLOCK_CHIPS:
        return part, []
    if step == 0:
        part = part[None, None]
    return part, [across(part, flip * (1 if step else 4)) for flip in FLIPS]


def spread_join(pair, step):
    part, others = pair
    if lax.axis_size("dp") != BLOCK_CHIPS:
        return part if step else lax.all_gather(part, "dp", axis=0, tiled=True)
    rank = lax.axis_index("dp")
    place = rank % 4 if step else rank // 4
    shape = part.shape[:step] + (4,) + part.shape[step + 1 :]
    whole = jnp.zeros(shape, part.dtype)
    for flip, piece in zip((0, *FLIPS), (part, *others)):
        whole = lax.dynamic_update_slice_in_dim(whole, piece, place ^ flip, step)
    return whole.reshape(-1, whole.shape[-1]) if step else whole


def gather_rows(shards):
    for step in range(4):
        shards = gather_step(shards, step)
    return shards


def reduce_send(parts, step):
    if lax.axis_size("dp") != BLOCK_CHIPS:
        if step > 0:
            return parts[0], []
        whole = jnp.concatenate(parts, axis=1)
        return lax.psum_scatter(whole, "dp", scatter_dimension=0, tiled=True), []
    rank = lax.axis_index("dp")
    place, unit = (rank // 4, 4) if step else (rank % 4, 1)
    if step == 0:
        parts = [part.reshape(4, 4, -1, part.shape[1]) for part in parts]

    def cut(flip):
        pieces = [
            lax.dynamic_slice_in_dim(part, place ^ flip, 1, axis=1 - step) for part in parts
        ]
        return pieces[0] if len(pieces) == 1 else jnp.concatenate(pieces, axis=-1)

    return cut(0), [across(cut(flip), flip * unit) for flip in FLIPS]


def reduce_add(pair, step):
    total = pair[0].astype(jnp.float32)
    for other in pair[1]:
        total = total + other.astype(jnp.float32)
    if lax.axis_size("dp") != BLOCK_CHIPS:
        return total
    return total.reshape(-1, total.shape[-1]) if step else total.astype(jnp.bfloat16)


def tied(transfer, computed):
    return lax.optimization_barrier((transfer, computed))


def in_order(mine, other, tensor_rank):
    return jnp.where(
        tensor_rank == 0,
        jnp.concatenate([mine, other], axis=0),
        jnp.concatenate([other, mine], axis=0),
    )


def split_sum(partial, tensor_rank):
    half = partial.shape[0] // 2
    keep = lax.dynamic_slice_in_dim(partial, tensor_rank * half, half, axis=0)
    send = lax.dynamic_slice_in_dim(partial, (1 - tensor_rank) * half, half, axis=0)
    return keep, partner(send)


def local(
    residual,
    cotangent,
    segment,
    expand,
    expand_first,
    expand_second,
    select,
    select_first,
    select_second,
    attention,
    attention_moment_one,
    attention_moment_two,
    project,
    project_first,
    project_second,
    combine,
    combine_first,
    combine_second,
    widening,
    widening_first,
    widening_second,
    narrowing,
    narrowing_first,
    narrowing_second,
    kernel,
    kernel_first,
    kernel_second,
    scales,
    scales_first,
    scales_second,
    decays,
    decays_first,
    decays_second,
):
    tensor_rank = lax.axis_index("tensor")
    width_local = expand.shape[2]
    heads_local = width_local // PD
    kv_local = attention.shape[1]
    width_ff = widening.shape[2]
    token_positions = token_places(segment)
    gain_first = scales[:MODEL_WIDTH]
    gain_second = scales[MODEL_WIDTH : 2 * MODEL_WIDTH]
    gain_inner = lax.dynamic_slice_in_dim(
        scales, 2 * MODEL_WIDTH + tensor_rank * width_local, width_local
    )
    taps_inner = lax.dynamic_slice_in_dim(kernel, tensor_rank * width_local, width_local, axis=1)
    taps_state = kernel[:, DSSM:]
    rates_local = lax.dynamic_slice_in_dim(decays, tensor_rank * heads_local, heads_local, axis=1)
    resid_float = residual.astype(jnp.float32)
    normed_input, first_back = jax.vjp(rms_apply, resid_float, gain_first)
    normed_low = normed_input.astype(jnp.bfloat16)
    normed_all = in_order(normed_low, partner(normed_low), tensor_rank)
    low = jnp.bfloat16
    rows_local = expand.shape[0]
    gate_weights, inner_weights, attention_weights = gather_rows(
        [
            expand[:, 0].astype(low),
            expand[:, 1].astype(low),
            attention.reshape(rows_local, -1).astype(low),
        ]
    )
    other_weights = lax.all_gather(
        jnp.concatenate(
            [
                project.T.astype(low),
                combine.T.astype(low),
                widening.reshape(rows_local, -1).astype(low),
                narrowing.T.astype(low),
            ],
            axis=1,
        ),
        "dp",
        axis=0,
        tiled=True,
    )
    width_mix = width_local + combine.shape[0]
    mix_out_weights = other_weights[:, :width_mix]
    widening_weights = other_weights[:, width_mix : width_mix + 2 * width_ff]
    narrowing_weights = other_weights[:, width_mix + 2 * width_ff :]
    select_low = select.astype(low)
    selected = product(normed_all, select_low)
    cosine, sine = rotary_tables(token_positions)
    marks = chunk_marks(segment, token_positions)
    seg_col, seg_row = marks[:2]
    log_rates, skip_gains, step_bias = rates_local
    step_raw = lax.dynamic_slice_in_dim(
        selected, 2 * NS + tensor_rank * heads_local, heads_local, axis=1
    )
    step_sizes, step_back = jax.vjp(lambda v, w: jax.nn.softplus(v + w), step_raw, step_bias)
    rates = -jnp.exp(log_rates)
    skip = jnp.repeat(skip_gains, PD)[None, :]
    packed_tokens = product(normed_all, attention_weights)
    attended = attend_forward(packed_tokens, cosine, sine, seg_col, seg_row)
    (inner_weights, gate_weights), attended = tied((inner_weights, gate_weights), attended)
    attended_low, rotated, peaks = attended
    inner = product(normed_all, inner_weights)
    gate_part = product(normed_all, gate_weights)
    ssd_inputs = (inner, selected, taps_inner, taps_state, skip, step_sizes, rates, marks)
    gated, y, squares, pre_inner, pre_state, kept_states = ssd_forward(*ssd_inputs, gate_part)
    square_sum = squares + partner(squares)
    spread_inverse = lax.rsqrt(square_sum / DSSM + EPSILON)
    inner_normed = gated * spread_inverse * gain_inner
    mixed_low = jnp.concatenate([inner_normed.astype(low), attended_low], axis=1)
    mixed_keep, mixed_other = split_sum(product_nt(mixed_low, mix_out_weights), tensor_rank)
    hidden = resid_float + (mixed_keep + mixed_other)
    normed_two, second_back = jax.vjp(rms_apply, hidden, gain_second)
    normed_two_low = normed_two.astype(low)
    normed_two_all = jnp.concatenate([normed_two_low, partner(normed_two_low)], axis=0)
    half_rows = residual.shape[0]
    gate_up = product(normed_two_all, widening_weights)
    gate_values = gate_up[:, :width_ff]
    up_values = gate_up[:, width_ff:]
    sigmoid_gate = jax.nn.sigmoid(gate_values)
    activated = (gate_values * sigmoid_gate * up_values).astype(jnp.bfloat16)
    ffn_part = product_nt(activated, narrowing_weights).astype(jnp.bfloat16)
    ffn_out = ffn_part[:half_rows].astype(jnp.float32) + partner(ffn_part[half_rows:]).astype(
        jnp.float32
    )
    output = (hidden + ffn_out).astype(jnp.bfloat16)
    cot_all = jnp.concatenate([cotangent, partner(cotangent)], axis=0)
    d_activated = product(cot_all, narrowing_weights)
    grad_narrowing = product_tn(cot_all, activated).astype(low)
    d_gate = (
        d_activated * up_values * (sigmoid_gate + gate_values * sigmoid_gate * (1.0 - sigmoid_gate))
    )
    d_up = d_activated * (gate_values * sigmoid_gate)
    d_gate_up = jnp.concatenate([d_gate, d_up], axis=1).astype(low)
    grad_widening = product_tn(normed_two_all, d_gate_up).astype(low)
    ffn_sent = reduce_send([grad_widening, grad_narrowing], 0)
    d_normed_two_part = product_nt(d_gate_up, widening_weights)
    d_normed_two = d_normed_two_part[:half_rows] + partner(d_normed_two_part[half_rows:])
    d_hidden_norm, grad_gain_second = second_back(d_normed_two)
    d_hidden = cotangent.astype(jnp.float32) + d_hidden_norm
    d_hidden_low = d_hidden.astype(low)
    d_hidden_all = in_order(d_hidden_low, partner(d_hidden_low), tensor_rank)
    d_mix_out = product(d_hidden_all, mix_out_weights)
    d_inner_normed = d_mix_out[:, :width_local]
    d_packed_low = attend_backward(
        rotated, peaks, d_mix_out[:, width_local:], cosine, sine, seg_col, seg_row
    )
    scaled_grad = d_inner_normed * gain_inner
    along = jnp.sum(scaled_grad * gated, axis=1, keepdims=True)
    along = along + partner(along)
    grad_gain_inner = jnp.sum(d_inner_normed * gated * spread_inverse, axis=0)
    d_gated = scaled_grad * spread_inverse - gated * (along * spread_inverse**3 / DSSM)
    sigmoid_part = jax.nn.sigmoid(gate_part)
    d_y = d_gated * (gate_part * sigmoid_part)
    d_gate_low = (
        d_gated * y * (sigmoid_part * (1.0 + gate_part * (1.0 - sigmoid_part)))
    ).astype(low)
    grad_mix_out = product_tn(d_hidden_all, mixed_low).astype(low)
    early_parts = [
        grad_mix_out,
        product_tn(normed_all, d_gate_low).astype(low),
        product_tn(normed_all, d_packed_low).astype(low),
    ]
    (ffn_sent, early_parts), back_rates = tied((ffn_sent, early_parts), rates)
    ffn_sent = reduce_send([reduce_add(ffn_sent, 0)], 1)
    early_sent = reduce_send(early_parts, 0)
    ssd_inputs = (*ssd_inputs[:-2], back_rates, marks)
    ssd_grads = ssd_backward(*ssd_inputs, pre_inner, pre_state, kept_states, d_y)
    ffn_sent, ssd_grads = tied(ffn_sent, ssd_grads)
    ffn_sum = reduce_add(ffn_sent, 1)
    d_inner_low, d_state_low, d_step_sizes, d_rates, grad_taps_inner, grad_taps_state, d_skip = (
        ssd_grads
    )
    d_step_raw, d_bias = step_back(d_step_sizes)
    grad_rates = jnp.stack(
        [
            jnp.sum(d_rates, axis=(0, 1)) * rates,
            jnp.sum(d_skip.reshape(heads_local, PD), axis=1),
            d_bias,
        ]
    )
    d_steps_low = lax.dynamic_update_slice_in_dim(
        jnp.zeros((segment.shape[0], selected.shape[1] - 2 * NS), low),
        d_step_raw.astype(low),
        tensor_rank * heads_local,
        axis=1,
    )
    d_selected_low = jnp.concatenate([d_state_low, d_steps_low], axis=1)
    grad_select = product_tn(normed_all, d_selected_low)
    kernel_grad = lax.dynamic_update_slice_in_dim(
        jnp.zeros_like(kernel), grad_taps_inner, tensor_rank * width_local, axis=1
    )
    kernel_grad = lax.dynamic_update_slice_in_dim(kernel_grad, grad_taps_state, DSSM, axis=1)
    decays_grad = lax.dynamic_update_slice_in_dim(
        jnp.zeros_like(decays), grad_rates, tensor_rank * heads_local, axis=1
    )
    inner_gain_grad = lax.dynamic_update_slice_in_dim(
        jnp.zeros((DSSM,), jnp.float32), grad_gain_inner, tensor_rank * width_local, axis=0
    )
    small = jnp.concatenate(
        [kernel_grad.reshape(-1), grad_gain_second, inner_gain_grad, decays_grad.reshape(-1)]
    )
    small_size = small.shape[0]
    small_columns = -(-small_size // MODEL_WIDTH)
    small = jnp.pad(small, (0, small_columns * MODEL_WIDTH - small_size))
    select_columns = select.shape[1]
    shared = jnp.concatenate(
        [grad_select, small.reshape(MODEL_WIDTH, small_columns)], axis=1
    ).astype(low)
    shared = jnp.pad(shared, ((0, 0), (0, -shared.shape[1] % 128)))
    shared_keep, shared_other = split_sum(shared, tensor_rank)
    shared_other, d_inner_low = tied(shared_other, d_inner_low)
    shared_sent = reduce_send([shared_keep + shared_other], 0)
    grad_inner = product_tn(normed_all, d_inner_low).astype(low)
    (shared_sent, early_sent), (grad_inner, d_selected_low) = tied(
        (shared_sent, early_sent), (grad_inner, d_selected_low)
    )
    shared_sent = reduce_send([reduce_add(shared_sent, 0)], 1)
    inner_sent = reduce_send([grad_inner], 0)
    early_sent = reduce_send([reduce_add(early_sent, 0)], 1)
    d_normed_part = (
        product_nt(d_gate_low, gate_weights)
        + product_nt(d_packed_low, attention_weights)
        + product_nt(d_inner_low, inner_weights)
        + product_nt(d_selected_low, select_low)
    ).astype(low)
    d_normed_keep, d_normed_other = split_sum(d_normed_part, tensor_rank)
    d_normed = d_normed_keep.astype(jnp.float32) + d_normed_other.astype(jnp.float32)
    d_resid_norm, grad_gain_first = first_back(d_normed)
    gradient = d_hidden + d_resid_norm
    lanes = shared.shape[1]
    gain_rows = 8
    gain_part = jnp.pad(grad_gain_first, (0, gain_rows * lanes - MODEL_WIDTH))
    gain_part = gain_part.reshape(gain_rows, lanes)
    shared_sent, gain_part = tied(shared_sent, gain_part)
    shared_rows = reduce_add(shared_sent, 1).astype(jnp.float32)
    shared_sent = spread_send(jnp.concatenate([shared_rows, gain_part], axis=0), 0)
    shared_sent, inner_sent = tied(shared_sent, inner_sent)
    shared_sent = spread_send(spread_join(shared_sent, 0), 1)
    inner_sent = reduce_send([reduce_add(inner_sent, 0)], 1)
    shared_sent, early_sent = tied(shared_sent, early_sent)
    shared_half = spread_join(shared_sent, 1).reshape(-1, shared_rows.shape[0] + gain_rows, lanes)
    gain_half = jnp.sum(shared_half[:, -gain_rows:], axis=0)
    shared_half = shared_half[:, :-gain_rows].reshape(-1, lanes)
    half = shared_half.shape[0]
    theirs = partner(jnp.concatenate([shared_half, gain_half], axis=0))
    shared = in_order(shared_half, theirs[:half], tensor_rank)
    gain_first_total = (gain_half + theirs[half:]).reshape(-1)[:MODEL_WIDTH]
    early_sum = reduce_add(early_sent, 1)
    inner_sum = reduce_add(inner_sent, 1)
    select_total = shared[:, :select_columns]
    small = shared[:, select_columns : select_columns + small_columns].reshape(-1)
    widening_sum = ffn_sum[:, : 2 * width_ff]
    narrowing_sum = ffn_sum[:, 2 * width_ff :]
    mix_out_sum = early_sum[:, :width_mix]
    gate_sum = early_sum[:, width_mix : width_mix + width_local]
    attention_sum = early_sum[:, width_mix + width_local :]
    large_grads = (
        jnp.stack([gate_sum, inner_sum], axis=1),
        attention_sum.reshape(attention.shape),
        widening_sum.reshape(widening.shape),
        mix_out_sum[:, :width_local].T,
        mix_out_sum[:, width_local:].T,
        narrowing_sum.T,
    )
    kernel_size = kernel.size
    kernel_total = small[:kernel_size].reshape(kernel.shape)
    rest = scales.shape[0] - MODEL_WIDTH
    scales_total = jnp.concatenate([gain_first_total, small[kernel_size : kernel_size + rest]])
    decays_total = small[kernel_size + rest : small_size].reshape(decays.shape)
    expand_mean, expand_square, expand_update = adam_step(
        expand, large_grads[0], expand_first, expand_second, RATE_MATRIX, WEIGHT_DECAY
    )
    select_mean, select_square, select_update = adam_step(
        select, select_total, select_first, select_second, RATE_MATRIX, WEIGHT_DECAY
    )
    attention_mean, attention_square, attention_update = adam_step(
        attention,
        large_grads[1],
        attention_moment_one,
        attention_moment_two,
        RATE_MATRIX,
        WEIGHT_DECAY,
    )
    project_mean, project_square, project_update = adam_step(
        project, large_grads[3], project_first, project_second, RATE_PROJECT, WEIGHT_DECAY
    )
    combine_mean, combine_square, combine_update = adam_step(
        combine, large_grads[4], combine_first, combine_second, RATE_COMBINE, WEIGHT_DECAY
    )
    widening_mean, widening_square, widening_update = adam_step(
        widening, large_grads[2], widening_first, widening_second, RATE_MATRIX, WEIGHT_DECAY
    )
    narrowing_mean, narrowing_square, narrowing_update = adam_step(
        narrowing, large_grads[5], narrowing_first, narrowing_second, RATE_NARROWING, WEIGHT_DECAY
    )
    kernel_mean, kernel_square, kernel_update = adam_step(
        kernel, kernel_total, kernel_first, kernel_second, RATE_KERNEL, 0.0
    )
    scales_mean, scales_square, scales_update = adam_step(
        scales, scales_total, scales_first, scales_second, RATE_SCALES, 0.0
    )
    decays_mean, decays_square, decays_update = adam_step(
        decays, decays_total, decays_first, decays_second, RATE_DECAYS, 0.0
    )
    return (
        output,
        gradient,
        expand_mean,
        expand_square,
        expand_update,
        select_mean,
        select_square,
        select_update,
        attention_mean,
        attention_square,
        attention_update,
        project_mean,
        project_square,
        project_update,
        combine_mean,
        combine_square,
        combine_update,
        widening_mean,
        widening_square,
        widening_update,
        narrowing_mean,
        narrowing_square,
        narrowing_update,
        kernel_mean,
        kernel_square,
        kernel_update,
        scales_mean,
        scales_square,
        scales_update,
        decays_mean,
        decays_square,
        decays_update,
    )


def solution(mesh):
    placed = (
        P(("dp", "tensor"), None),
        P(("dp", "tensor"), None),
        P("dp"),
        P("dp", None, "tensor"),
        P("dp", None, "tensor"),
        P("dp", None, "tensor"),
        P(),
        P(),
        P(),
        P("dp", "tensor", None),
        P("dp", "tensor", None),
        P("dp", "tensor", None),
        P("tensor", "dp"),
        P("tensor", "dp"),
        P("tensor", "dp"),
        P("tensor", "dp"),
        P("tensor", "dp"),
        P("tensor", "dp"),
        P("dp", None, "tensor"),
        P("dp", None, "tensor"),
        P("dp", None, "tensor"),
        P("tensor", "dp"),
        P("tensor", "dp"),
        P("tensor", "dp"),
        P(),
        P(),
        P(),
        P(),
        P(),
        P(),
        P(),
        P(),
        P(),
    )
    return jax.shard_map(
        local,
        mesh=mesh,
        in_specs=placed,
        out_specs=(
            P(("dp", "tensor"), None),
            P(("dp", "tensor"), None),
            P("dp", None, "tensor"),
            P("dp", None, "tensor"),
            P("dp", None, "tensor"),
            P(),
            P(),
            P(),
            P("dp", "tensor", None),
            P("dp", "tensor", None),
            P("dp", "tensor", None),
            P("tensor", "dp"),
            P("tensor", "dp"),
            P("tensor", "dp"),
            P("tensor", "dp"),
            P("tensor", "dp"),
            P("tensor", "dp"),
            P("dp", None, "tensor"),
            P("dp", None, "tensor"),
            P("dp", None, "tensor"),
            P("tensor", "dp"),
            P("tensor", "dp"),
            P("tensor", "dp"),
            P(),
            P(),
            P(),
            P(),
            P(),
            P(),
            P(),
            P(),
            P(),
        ),
        check_vma=False,
    )
```
